512 devices in a mesh: dp: 32 (over z, core), tensor: 16 (over y, x).
Axes of the slice: x: 4, y: 4, z: 16, core: 2. Of those that a mesh axis runs over, the one named last changes fastest.
Arguments:
- gradients: bfloat16 [32, 512, 4096], P('dp', None, 'tensor'), may hold values from -12 to 12
- momentum: float32 [512, 4096], P('dp', 'tensor'), may hold values from -16 to 16
- weight: float32 [512, 4096], P('dp', 'tensor'), may hold values from -0.25 to 0.25
Outputs:
- new_momentum: float32 [512, 4096], P('dp', 'tensor')
- new_weight: float32 [512, 4096], P('dp', 'tensor')
- residual: float32 [512, 512], P('dp', 'tensor')
The draws below stay inside these ranges and needn't reach their ends.
All inputs are finite; a program needn't handle non-finite values.
Results may differ from the reference program's by a relative error of at most 0.0003.
Values sent between devices are 32-bit elements; how exact they have to be, the bound alone decides.
No kernel may reach another device: no remote copies, remote signals or barrier semaphores. Data moves between devices by JAX's collectives and lax.ppermute only.
A program may use at most 64 MiB of HBM per device.

```python
import jax
import jax.numpy as jnp
from jax import lax

IN = 512
OUT = 4096
ITERS = 2
N_DP = 32


def with_spikes(values, stream_key, source, target, shards_of, factor):
    owner, partner = [(jnp.arange(values.shape[position]) // (values.shape[position] // shards_of)).reshape([-1 if axis == position else 1 for axis in range(values.ndim)]) for position in (source, target)]
    chosen = jax.random.permutation(stream_key, shards_of)[partner]
    strong = (owner == chosen) | (owner == (partner + shards_of // 2) % shards_of)
    return jnp.where(strong, factor * values, values)


def shard_levels(key, dims, shards, low, top_value):
    def one(axis_at, blocks):
        heights = jax.random.uniform(jax.random.fold_in(jax.random.fold_in(key, 6), axis_at), (blocks,), jnp.float32, low / len(shards), top_value / len(shards))
        return jnp.repeat(jnp.exp(heights), dims[axis_at] // blocks).reshape((-1,) + (1,) * (len(dims) - axis_at - 1))

    factor_of = one(*shards[0])
    for cut in shards[1:]:
        factor_of = factor_of * one(*cut)
    return factor_of


def bell_draw(key, shape, deviation, limit, shards=(), kind=jnp.bfloat16):
    entries = deviation * jax.random.normal(key, shape, jnp.float32)
    if shards:
        entries = entries * shard_levels(key, shape, shards, -0.22, 0.18)
    return jnp.clip(entries, -limit, limit).astype(kind)


def bell_draw_with(key, shape, scale, most, split, heavy, held_as=jnp.bfloat16):
    array = scale * jax.random.normal(key, shape, jnp.float32)
    if split:
        array = array * shard_levels(key, shape, split, -0.22, 0.18)
    return jnp.clip(with_spikes(array, jax.random.fold_in(key, 3), *heavy), -most, most).astype(held_as)


def setup_inputs(seed: int = 0) -> dict:
    key_of = jax.random.split(jax.random.key(seed), 4)
    return {
        "gradients": bell_draw_with(key_of[0], (N_DP, IN, OUT), 1.0, 12.0, ((0, 32), (2, 16)), (0, 1, 32, 2.75)),
        "momentum": bell_draw(key_of[1], (IN, OUT), 3.0, 16.0, ((0, 32), (1, 16)), jnp.float32),
        "weight": bell_draw(key_of[2], (IN, OUT), IN ** -0.5, 0.25, ((0, 32), (1, 16)), jnp.float32),
    }


decay_rate = 0.95
learn_rate = 0.02
weight_decay = 0.1
epsilon = 1e-07
quintic_a = 3.4445
quintic_b = -4.775
quintic_c = 2.0315

def reference(gradients, momentum, weight):
    summed = lax.optimization_barrier(jnp.sum(gradients.astype(jnp.float32), axis=0))
    new_momentum = decay_rate * momentum + summed
    squares = jnp.sum(new_momentum * new_momentum)
    iterate = new_momentum / (jnp.sqrt(squares) + epsilon)
    for sweep in range(ITERS):
        gram_mat = jnp.dot(iterate, iterate.T, precision=lax.Precision.HIGHEST)
        product_one = jnp.dot(gram_mat, iterate, precision=lax.Precision.HIGHEST)
        product_two = jnp.dot(gram_mat, product_one, precision=lax.Precision.HIGHEST)
        iterate = quintic_a * iterate + quintic_b * product_one + quintic_c * product_two
    scale_factor = 0.2 * jnp.sqrt(jnp.float32(max(IN, OUT)))
    new_weight = weight * (1.0 - learn_rate * weight_decay) - learn_rate * scale_factor * iterate
    residual = jnp.dot(iterate, iterate.T, precision=lax.Precision.HIGHEST) - jnp.eye(IN, dtype=jnp.float32)
    return (new_momentum, new_weight, residual)
```

```python
import jax
import jax.numpy as jnp
from jax import lax
from jax.experimental import pallas as pl
from jax.experimental.pallas import tpu as pltpu
from jax.sharding import PartitionSpec as P

IN = 512
OUT = 4096

decay_rate = 0.95
learn_rate = 0.02
weight_decay = 0.1
epsilon = 1e-07
quintic_a = 3.4445
quintic_b = -4.775
quintic_c = 2.0315

f32 = jnp.float32
bf16 = jnp.bfloat16

CORE = [(i, i ^ 1) for i in range(32)]
NEAR = [[8 * far + 2 * near + core for near in range(4)] for far in range(4) for core in range(2)]
FAR = [[8 * far + 2 * near + core for far in range(4)] for near in range(4) for core in range(2)]

NT = (((1,), (1,)), ((), ()))
NN = (((1,), (0,)), ((), ()))


def place():
    index = lax.axis_index("dp")
    return index // 8, (index // 2) % 4, index % 2


def halves(value):
    high = value.astype(bf16)
    low = (value - high.astype(f32)).astype(bf16)
    return high, low


def mul3(left, right, dims):
    dot = lambda x, y: lax.dot_general(x, y, dims, preferred_element_type=f32)
    return dot(left[0], right[0]) + (dot(left[0], right[1]) + dot(left[1], right[0]))


def split_kernel(grad_ref, keep_ref, send_ref):
    _, _, core = place()
    for far in range(4):
        for near in range(4):
            keep_ref[near, far] = grad_ref[far, near, core].astype(f32)
            send_ref[near, far] = grad_ref[far, near, 1 - core].astype(f32)


def near_sum_kernel(parts_ref, momentum_ref, out_ref):
    mine, _, _ = place()
    for far in range(4):
        total = (parts_ref[0, far] + parts_ref[1, far]) + (parts_ref[2, far] + parts_ref[3, far])
        total = total + jnp.where(mine == far, f32(decay_rate), f32(0.0)) * momentum_ref[...]
        for other in range(4):
            out_ref[other, far] = total


def far_sum_kernel(parts_ref, out_ref, momentum_ref):
    mine, _, _ = place()
    for far in range(4):
        total = (parts_ref[0, far] + parts_ref[1, far]) + (parts_ref[2, far] + parts_ref[3, far])
        for other in range(4):
            out_ref[other, far] = total
    momentum_ref[...] = out_ref[0, mine]


def gram_kernel(mine_ref, other_ref, out_ref, rows_ref):
    _, _, core = place()
    rows_ref[core] = mine_ref[...]
    rows_ref[1 - core] = other_ref[...]
    own = halves(mine_ref[...])
    upper = tuple(part[:128] for part in own)
    lower = tuple(part[128:] for part in own)
    out_ref[0:128] = mul3(upper, upper, NT)
    out_ref[128:256] = mul3(upper, lower, NT)
    out_ref[256:384] = mul3(lower, lower, NT)
    left = halves(rows_ref[0])
    right = halves(rows_ref[1, pl.ds(pl.multiple_of(core * 128, 128), 128)])
    out_ref[384:640] = mul3(left, right, NT)


def tensor_sum_kernel(parts_ref, out_ref):
    total = parts_ref[0]
    for index in range(1, 16):
        total = total + parts_ref[index]
    for index in range(16):
        out_ref[index] = total


def diagonal(start_row, start_column, shape):
    rows = start_row + lax.broadcasted_iota(jnp.int32, shape, 0)
    columns = start_column + lax.broadcasted_iota(jnp.int32, shape, 1)
    return rows == columns


def final_kernel(mine_ref, other_ref, rows_ref, weight_ref, new_weight_ref, residual_ref, gram_ref, first_ref, next_ref):
    far, near, core = place()
    tensor = lax.axis_index("tensor")
    for which in range(2):
        pick = core == which
        block = lambda start, size: jnp.where(pick, mine_ref[start : start + size], other_ref[start : start + size])
        base = 256 * which
        corner = block(128, 128)
        gram_ref[base : base + 128, base : base + 128] = block(0, 128)
        gram_ref[base : base + 128, base + 128 : base + 256] = corner
        gram_ref[base + 128 : base + 256, base : base + 128] = corner.T
        gram_ref[base + 128 : base + 256, base + 128 : base + 256] = block(256, 128)
        cross = block(384, 256)
        start = 256 + 128 * which
        gram_ref[0:256, start : start + 128] = cross
        gram_ref[start : start + 128, 0:256] = cross.T
    unit = diagonal(0, 0, (IN, IN))
    whole = gram_ref[...]
    squares = jnp.sum(jnp.sum(jnp.where(unit, whole, 0.0), axis=1, keepdims=True), axis=0, keepdims=True)
    inverse = 1.0 / (jnp.sqrt(squares) + epsilon)
    gram = (whole * inverse) * inverse
    pair = halves(gram)
    first = quintic_b * gram + quintic_c * mul3(pair, pair, NN) + jnp.where(unit, f32(quintic_a), f32(0.0))
    first_ref[...] = first
    first_pair = halves(first)
    inner = mul3(first_pair, pair, NN)
    after = mul3(first_pair, halves(inner), NN)
    next_ref[...] = after
    after_pair = halves(after)
    mine = core * 256 + near * 64 + far * 16
    column_base = lax.rem(tensor, 4) * 64 + lax.div(tensor, 4) * 16
    starts = (mine, column_base, 256 + column_base)
    bands = [next_ref[pl.ds(pl.multiple_of(start, 16), 16)] for start in starts]
    slab = jnp.concatenate(bands, axis=0)
    units = jnp.concatenate([diagonal(start, 0, (16, IN)) for start in starts], axis=0)
    second = quintic_b * slab + quintic_c * mul3(halves(slab), after_pair, NN) + jnp.where(units, f32(quintic_a), f32(0.0))
    own = halves(second[0:16])
    total = mul3(own, first_pair, NN)
    rows = rows_ref[...].reshape(IN, 256)
    update = mul3(halves(total), halves(rows), NN) * inverse
    scale = learn_rate * 0.2 * float(max(IN, OUT)) ** 0.5
    new_weight_ref[...] = weight_ref[...] * (1.0 - learn_rate * weight_decay) - scale * update
    product = mul3(own, after_pair, NN)
    final = mul3(halves(product), halves(second[16:48]), NT)
    identity = diagonal((far * 8 + near * 2 + core) * 16, tensor * 32, (16, 32))
    residual_ref[...] = final - jnp.where(identity, f32(1.0), f32(0.0))


def call(kernel, outs, scratch=(), limit=None):
    params = pltpu.CompilerParams(vmem_limit_bytes=limit) if limit else None
    return pl.pallas_call(
        kernel,
        out_shape=tuple(jax.ShapeDtypeStruct(shape, f32) for shape in outs),
        scratch_shapes=list(scratch),
        compiler_params=params,
    )


def exchange(value, axis, groups=None):
    return lax.all_to_all(value, axis, 0, 0, tiled=True, axis_index_groups=groups)


def per_device(gradients, momentum, weight):
    chunks = (4, 4, 16, 256)
    keep, send = call(split_kernel, [chunks, chunks])(gradients.reshape(4, 4, 2, 16, 256))
    parts = keep + lax.ppermute(send, "dp", CORE)
    (spread,) = call(near_sum_kernel, [chunks])(exchange(parts, "dp", NEAR), momentum)
    spread, new_momentum = call(far_sum_kernel, [chunks, (16, 256)])(exchange(spread, "dp", FAR))
    mine = exchange(spread, "dp", NEAR).reshape(256, 256)
    other = lax.ppermute(mine, "dp", CORE)
    blocks, rows = call(gram_kernel, [(640, 128), (2, 256, 256)], limit=32 << 20)(mine, other)
    (spread,) = call(tensor_sum_kernel, [(16, 40, 128)])(exchange(blocks.reshape(16, 40, 128), "tensor"))
    mine = exchange(spread, "tensor").reshape(640, 128)
    other = lax.ppermute(mine, "dp", CORE)
    new_weight, residual = call(
        final_kernel,
        [(16, 256), (16, 32)],
        [pltpu.VMEM((IN, IN), f32)] * 3,
        limit=48 << 20,
    )(mine, other, rows, weight)
    return (new_momentum, new_weight, residual)


def solution(mesh):
    return jax.shard_map(
        per_device,
        mesh=mesh,
        in_specs=(P("dp", None, "tensor"), P("dp", "tensor"), P("dp", "tensor")),
        out_specs=(P("dp", "tensor"), P("dp", "tensor"), P("dp", "tensor")),
        check_vma=False,
    )
```

```python
import jax
import jax.numpy as jnp
from jax import lax
from jax.experimental import pallas as pl
from jax.experimental.pallas import tpu as pltpu
from jax.sharding import PartitionSpec as P

IN = 512
OUT = 4096

decay_rate = 0.95
learn_rate = 0.02
weight_decay = 0.1
epsilon = 1e-07
quintic_a = 3.4445
quintic_b = -4.775
quintic_c = 2.0315

f32 = jnp.float32
bf16 = jnp.bfloat16

CORE = [(i, i ^ 1) for i in range(32)]
NEAR = [[8 * far + 2 * near + core for near in range(4)] for far in range(4) for core in range(2)]
FAR = [[8 * far + 2 * near + core for far in range(4)] for near in range(4) for core in range(2)]

NT = (((1,), (1,)), ((), ()))
NN = (((1,), (0,)), ((), ()))


def place():
    index = lax.axis_index("dp")
    return index // 8, (index // 2) % 4, index % 2


def halves(value):
    high = value.astype(bf16)
    low = (value - high.astype(f32)).astype(bf16)
    return high, low


def mul3(left, right, dims):
    dot = lambda x, y: lax.dot_general(x, y, dims, preferred_element_type=f32)
    return dot(left[0], right[0]) + (dot(left[0], right[1]) + dot(left[1], right[0]))


def send_kernel(grad_ref, send_ref):
    _, _, core = place()
    for far in range(4):
        for near in range(4):
            send_ref[near, far] = grad_ref[far, near, 1 - core].astype(f32)


def core_sum_kernel(grad_ref, got_ref, out_ref):
    _, _, core = place()
    for far in range(4):
        for near in range(4):
            out_ref[near, far] = grad_ref[far, near, core].astype(f32) + got_ref[near, far]


def near_sum_kernel(parts_ref, momentum_ref, out_ref):
    mine, _, _ = place()
    for far in range(4):
        total = (parts_ref[0, far] + parts_ref[1, far]) + (parts_ref[2, far] + parts_ref[3, far])
        total = total + jnp.where(mine == far, f32(decay_rate), f32(0.0)) * momentum_ref[...]
        for other in range(4):
            out_ref[other, far] = total


def far_sum_kernel(parts_ref, out_ref, momentum_ref):
    mine, _, _ = place()
    for far in range(4):
        total = (parts_ref[0, far] + parts_ref[1, far]) + (parts_ref[2, far] + parts_ref[3, far])
        for other in range(4):
            out_ref[other, far] = total
    momentum_ref[...] = out_ref[0, mine]


def gram_kernel(mine_ref, other_ref, out_ref, rows_ref):
    _, _, core = place()
    rows_ref[core] = mine_ref[...]
    rows_ref[1 - core] = other_ref[...]
    own = halves(mine_ref[...])
    upper = tuple(part[:128] for part in own)
    lower = tuple(part[128:] for part in own)
    out_ref[0:128] = mul3(upper, upper, NT)
    out_ref[128:256] = mul3(upper, lower, NT)
    out_ref[256:384] = mul3(lower, lower, NT)
    left = halves(rows_ref[0])
    right = halves(rows_ref[1, pl.ds(pl.multiple_of(core * 128, 128), 128)])
    out_ref[384:640] = mul3(left, right, NT)


def tensor_sum_kernel(parts_ref, out_ref):
    total = parts_ref[0]
    for index in range(1, 16):
        total = total + parts_ref[index]
    for index in range(16):
        out_ref[index] = total


def diagonal(start_row, start_column, shape):
    rows = start_row + lax.broadcasted_iota(jnp.int32, shape, 0)
    columns = start_column + lax.broadcasted_iota(jnp.int32, shape, 1)
    return rows == columns


def final_kernel(mine_ref, other_ref, rows_ref, weight_ref, new_weight_ref, residual_ref, gram_ref, first_ref, next_ref):
    far, near, core = place()
    tensor = lax.axis_index("tensor")
    for which in range(2):
        pick = core == which
        block = lambda start, size: jnp.where(pick, mine_ref[start : start + size], other_ref[start : start + size])
        base = 256 * which
        corner = block(128, 128)
        gram_ref[base : base + 128, base : base + 128] = block(0, 128)
        gram_ref[base : base + 128, base + 128 : base + 256] = corner
        gram_ref[base + 128 : base + 256, base : base + 128] = corner.T
        gram_ref[base + 128 : base + 256, base + 128 : base + 256] = block(256, 128)
        cross = block(384, 256)
        start = 256 + 128 * which
        gram_ref[0:256, start : start + 128] = cross
        gram_ref[start : start + 128, 0:256] = cross.T
    unit = diagonal(0, 0, (IN, IN))
    whole = gram_ref[...]
    squares = jnp.sum(jnp.sum(jnp.where(unit, whole, 0.0), axis=1, keepdims=True), axis=0, keepdims=True)
    inverse = 1.0 / (jnp.sqrt(squares) + epsilon)
    gram = (whole * inverse) * inverse
    pair = halves(gram)
    first = quintic_b * gram + quintic_c * mul3(pair, pair, NN) + jnp.where(unit, f32(quintic_a), f32(0.0))
    first_ref[...] = first
    first_pair = halves(first)
    inner = mul3(first_pair, pair, NN)
    after = mul3(first_pair, halves(inner), NN)
    next_ref[...] = after
    after_pair = halves(after)
    mine = core * 256 + near * 64 + far * 16
    column_base = lax.rem(tensor, 4) * 64 + lax.div(tensor, 4) * 16
    starts = (mine, column_base, 256 + column_base)
    bands = [next_ref[pl.ds(pl.multiple_of(start, 16), 16)] for start in starts]
    slab = jnp.concatenate(bands, axis=0)
    units = jnp.concatenate([diagonal(start, 0, (16, IN)) for start in starts], axis=0)
    second = quintic_b * slab + quintic_c * mul3(halves(slab), after_pair, NN) + jnp.where(units, f32(quintic_a), f32(0.0))
    own = halves(second[0:16])
    total = mul3(own, first_pair, NN)
    rows = rows_ref[...].reshape(IN, 256)
    update = mul3(halves(total), halves(rows), NN) * inverse
    scale = learn_rate * 0.2 * float(max(IN, OUT)) ** 0.5
    new_weight_ref[...] = weight_ref[...] * (1.0 - learn_rate * weight_decay) - scale * update
    product = mul3(own, after_pair, NN)
    final = mul3(halves(product), halves(second[16:48]), NT)
    identity = diagonal((far * 8 + near * 2 + core) * 16, tensor * 32, (16, 32))
    residual_ref[...] = final - jnp.where(identity, f32(1.0), f32(0.0))


def call(kernel, outs, scratch=(), limit=4 << 20):
    return pl.pallas_call(
        kernel,
        out_shape=tuple(jax.ShapeDtypeStruct(shape, f32) for shape in outs),
        scratch_shapes=list(scratch),
        compiler_params=pltpu.CompilerParams(vmem_limit_bytes=limit),
    )


def exchange(value, axis, groups=None):
    return lax.all_to_all(value, axis, 0, 0, tiled=True, axis_index_groups=groups)


def per_device(gradients, momentum, weight):
    chunks = (4, 4, 16, 256)
    gradients = gradients.reshape(4, 4, 2, 16, 256)
    (send,) = call(send_kernel, [chunks])(gradients)
    (parts,) = call(core_sum_kernel, [chunks])(gradients, lax.ppermute(send, "dp", CORE))
    (spread,) = call(near_sum_kernel, [chunks])(exchange(parts, "dp", NEAR), momentum)
    spread, new_momentum = call(far_sum_kernel, [chunks, (16, 256)])(exchange(spread, "dp", FAR))
    mine = exchange(spread, "dp", NEAR).reshape(256, 256)
    other = lax.ppermute(mine, "dp", CORE)
    blocks, rows = call(gram_kernel, [(640, 128), (2, 256, 256)], limit=8 << 20)(mine, other)
    (spread,) = call(tensor_sum_kernel, [(16, 40, 128)])(exchange(blocks.reshape(16, 40, 128), "tensor"))
    mine = exchange(spread, "tensor").reshape(640, 128)
    other = lax.ppermute(mine, "dp", CORE)
    new_weight, residual = call(
        final_kernel,
        [(16, 256), (16, 32)],
        [pltpu.VMEM((IN, IN), f32)] * 3,
        limit=24 << 20,
    )(mine, other, rows, weight)
    return (new_momentum, new_weight, residual)


def solution(mesh):
    return jax.shard_map(
        per_device,
        mesh=mesh,
        in_specs=(P("dp", None, "tensor"), P("dp", "tensor"), P("dp", "tensor")),
        out_specs=(P("dp", "tensor"), P("dp", "tensor"), P("dp", "tensor")),
        check_vma=False,
    )
```

```python
import jax
import jax.numpy as jnp
from jax import lax
from jax.experimental import pallas as pl
from jax.experimental.pallas import tpu as pltpu
from jax.sharding import PartitionSpec as P

IN = 512
OUT = 4096

decay_rate = 0.95
learn_rate = 0.02
weight_decay = 0.1
epsilon = 1e-07
quintic_a = 3.4445
quintic_b = -4.775
quintic_c = 2.0315

f32 = jnp.float32
bf16 = jnp.bfloat16

CORE = [(i, i ^ 1) for i in range(32)]
CHIPS = [[2 * chip + core for chip in range(16)] for core in range(2)]

NT = (((1,), (1,)), ((), ()))
NN = (((1,), (0,)), ((), ()))


def place():
    index = lax.axis_index("dp")
    return index // 2, index % 2


def halves(value):
    high = value.astype(bf16)
    low = (value - high.astype(f32)).astype(bf16)
    return high, low


def mul3(left, right, dims):
    dot = lambda x, y: lax.dot_general(x, y, dims, preferred_element_type=f32)
    return dot(left[0], right[0]) + (dot(left[0], right[1]) + dot(left[1], right[0]))


def send_kernel(grad_ref, send_ref):
    _, core = place()
    for chip in range(16):
        send_ref[chip] = grad_ref[chip, 1 - core].astype(f32)


def core_sum_kernel(grad_ref, got_ref, out_ref):
    _, core = place()
    for chip in range(16):
        out_ref[chip] = grad_ref[chip, core].astype(f32) + got_ref[chip]


def chip_sum_kernel(parts_ref, momentum_ref, out_ref, new_momentum_ref):
    total = parts_ref[0]
    for chip in range(1, 16):
        total = total + parts_ref[chip]
    total = decay_rate * momentum_ref[...] + total
    new_momentum_ref[...] = total
    for chip in range(16):
        out_ref[chip] = total


def gram_kernel(mine_ref, other_ref, out_ref, rows_ref):
    _, core = place()
    rows_ref[core] = mine_ref[...]
    rows_ref[1 - core] = other_ref[...]
    own = halves(mine_ref[...])
    upper = tuple(part[:128] for part in own)
    lower = tuple(part[128:] for part in own)
    out_ref[0:128] = mul3(upper, upper, NT)
    out_ref[128:256] = mul3(upper, lower, NT)
    out_ref[256:384] = mul3(lower, lower, NT)
    left = halves(rows_ref[0])
    right = halves(rows_ref[1, pl.ds(pl.multiple_of(core * 128, 128), 128)])
    out_ref[384:640] = mul3(left, right, NT)


def tensor_sum_kernel(parts_ref, out_ref):
    total = parts_ref[0]
    for index in range(1, 16):
        total = total + parts_ref[index]
    for index in range(16):
        out_ref[index] = total


def diagonal(start_row, start_column, shape):
    rows = start_row + lax.broadcasted_iota(jnp.int32, shape, 0)
    columns = start_column + lax.broadcasted_iota(jnp.int32, shape, 1)
    return rows == columns


def final_kernel(mine_ref, other_ref, rows_ref, weight_ref, new_weight_ref, residual_ref, gram_ref, first_ref, next_ref):
    chip, core = place()
    tensor = lax.axis_index("tensor")
    for which in range(2):
        pick = core == which
        block = lambda start, size: jnp.where(pick, mine_ref[start : start + size], other_ref[start : start + size])
        base = 256 * which
        corner = block(128, 128)
        gram_ref[base : base + 128, base : base + 128] = block(0, 128)
        gram_ref[base : base + 128, base + 128 : base + 256] = corner
        gram_ref[base + 128 : base + 256, base : base + 128] = corner.T
        gram_ref[base + 128 : base + 256, base + 128 : base + 256] = block(256, 128)
        cross = block(384, 256)
        start = 256 + 128 * which
        gram_ref[0:256, start : start + 128] = cross
        gram_ref[start : start + 128, 0:256] = cross.T
    unit = diagonal(0, 0, (IN, IN))
    whole = gram_ref[...]
    squares = jnp.sum(jnp.sum(jnp.where(unit, whole, 0.0), axis=1, keepdims=True), axis=0, keepdims=True)
    inverse = 1.0 / (jnp.sqrt(squares) + epsilon)
    gram = (whole * inverse) * inverse
    pair = halves(gram)
    first = quintic_b * gram + quintic_c * mul3(pair, pair, NN) + jnp.where(unit, f32(quintic_a), f32(0.0))
    first_ref[...] = first
    first_pair = halves(first)
    inner = mul3(first_pair, pair, NN)
    after = mul3(first_pair, halves(inner), NN)
    next_ref[...] = after
    after_pair = halves(after)
    starts = (core * 256 + chip * 16, tensor * 16, 256 + tensor * 16)
    bands = [next_ref[pl.ds(pl.multiple_of(start, 16), 16)] for start in starts]
    slab = jnp.concatenate(bands, axis=0)
    units = jnp.concatenate([diagonal(start, 0, (16, IN)) for start in starts], axis=0)
    second = quintic_b * slab + quintic_c * mul3(halves(slab), after_pair, NN) + jnp.where(units, f32(quintic_a), f32(0.0))
    own = halves(second[0:16])
    total = mul3(own, first_pair, NN)
    rows = rows_ref[...].reshape(IN, 256)
    update = mul3(halves(total), halves(rows), NN) * inverse
    scale = learn_rate * 0.2 * float(max(IN, OUT)) ** 0.5
    new_weight_ref[...] = weight_ref[...] * (1.0 - learn_rate * weight_decay) - scale * update
    product = mul3(own, after_pair, NN)
    final = mul3(halves(product), halves(second[16:48]), NT)
    identity = diagonal((chip * 2 + core) * 16, tensor * 32, (16, 32))
    residual_ref[...] = final - jnp.where(identity, f32(1.0), f32(0.0))


def call(kernel, outs, scratch=(), limit=4 << 20):
    return pl.pallas_call(
        kernel,
        out_shape=tuple(jax.ShapeDtypeStruct(shape, f32) for shape in outs),
        scratch_shapes=list(scratch),
        compiler_params=pltpu.CompilerParams(vmem_limit_bytes=limit),
    )


def exchange(value, axis, groups=None):
    return lax.all_to_all(value, axis, 0, 0, tiled=True, axis_index_groups=groups)


def per_device(gradients, momentum, weight):
    chunks = (16, 16, 256)
    gradients = gradients.reshape(16, 2, 16, 256)
    (send,) = call(send_kernel, [chunks])(gradients)
    (parts,) = call(core_sum_kernel, [chunks])(gradients, lax.ppermute(send, "dp", CORE))
    spread, new_momentum = call(chip_sum_kernel, [chunks, (16, 256)])(exchange(parts, "dp", CHIPS), momentum)
    mine = exchange(spread, "dp", CHIPS).reshape(256, 256)
    other = lax.ppermute(mine, "dp", CORE)
    blocks, rows = call(gram_kernel, [(640, 128), (2, 256, 256)], limit=8 << 20)(mine, other)
    (spread,) = call(tensor_sum_kernel, [(16, 40, 128)])(exchange(blocks.reshape(16, 40, 128), "tensor"))
    mine = exchange(spread, "tensor").reshape(640, 128)
    other = lax.ppermute(mine, "dp", CORE)
    new_weight, residual = call(
        final_kernel,
        [(16, 256), (16, 32)],
        [pltpu.VMEM((IN, IN), f32)] * 3,
        limit=24 << 20,
    )(mine, other, rows, weight)
    return (new_momentum, new_weight, residual)


def solution(mesh):
    return jax.shard_map(
        per_device,
        mesh=mesh,
        in_specs=(P("dp", None, "tensor"), P("dp", "tensor"), P("dp", "tensor")),
        out_specs=(P("dp", "tensor"), P("dp", "tensor"), P("dp", "tensor")),
        check_vma=False,
    )
```

```python
import jax
import jax.numpy as jnp
from jax import lax
from jax.experimental import pallas as pl
from jax.experimental.pallas import tpu as pltpu
from jax.sharding import PartitionSpec as P

IN = 512
OUT = 4096

decay_rate = 0.95
learn_rate = 0.02
weight_decay = 0.1
epsilon = 1e-07
quintic_a = 3.4445
quintic_b = -4.775
quintic_c = 2.0315

f32 = jnp.float32
bf16 = jnp.bfloat16


def chip_of(near, far, core):
    return (4 * far + near + 2 * core) % 16


def index_of(near, far, core):
    return 2 * chip_of(near, far, core) + core


CORE = [(i, i ^ 1) for i in range(32)]
NEAR = [[index_of(near, far, core) for near in range(4)] for far in range(4) for core in range(2)]
FAR = [[index_of(near, far, core) for far in range(4)] for near in range(4) for core in range(2)]

NT = (((1,), (1,)), ((), ()))
NN = (((1,), (0,)), ((), ()))


def place():
    index = lax.axis_index("dp")
    core = lax.rem(index, 2)
    spot = lax.rem(lax.div(index, 2) + 16 - 2 * core, 16)
    return lax.rem(spot, 4), lax.div(spot, 4), core


def halves(value):
    high = value.astype(bf16)
    low = (value - high.astype(f32)).astype(bf16)
    return high, low


def mul3(left, right, dims):
    dot = lambda x, y: lax.dot_general(x, y, dims, preferred_element_type=f32)
    return dot(left[0], right[0]) + (dot(left[0], right[1]) + dot(left[1], right[0]))


def send_kernel(grad_ref, send_ref):
    _, _, core = place()
    other = 1 - core
    for near in range(4):
        for far in range(4):
            send_ref[near, far] = grad_ref[lax.rem(4 * far + near + 2 * other, 16), other].astype(f32)


def core_sum_kernel(grad_ref, got_ref, out_ref):
    _, _, core = place()
    for near in range(4):
        for far in range(4):
            rows = grad_ref[lax.rem(4 * far + near + 2 * core, 16), core].astype(f32)
            out_ref[near, far] = rows + got_ref[near, far]


def near_sum_kernel(parts_ref, momentum_ref, out_ref):
    _, mine, _ = place()
    for far in range(4):
        total = (parts_ref[0, far] + parts_ref[1, far]) + (parts_ref[2, far] + parts_ref[3, far])
        total = total + jnp.where(mine == far, f32(decay_rate), f32(0.0)) * momentum_ref[...]
        for other in range(4):
            out_ref[other, far] = total


def far_sum_kernel(parts_ref, out_ref):
    for far in range(4):
        total = (parts_ref[0, far] + parts_ref[1, far]) + (parts_ref[2, far] + parts_ref[3, far])
        for other in range(4):
            out_ref[other, far] = total


def gram_kernel(mine_ref, other_ref, out_ref, rows_ref):
    _, _, core = place()
    rows_ref[core] = mine_ref[...]
    rows_ref[1 - core] = other_ref[...]
    own = halves(mine_ref[...])
    upper = tuple(part[:128] for part in own)
    lower = tuple(part[128:] for part in own)
    out_ref[0:128] = mul3(upper, upper, NT)
    out_ref[128:256] = mul3(upper, lower, NT)
    out_ref[256:384] = mul3(lower, lower, NT)
    left = halves(rows_ref[0])
    right = halves(rows_ref[1, pl.ds(pl.multiple_of(core * 128, 128), 128)])
    out_ref[384:640] = mul3(left, right, NT)


def tensor_sum_kernel(parts_ref, out_ref):
    total = parts_ref[0]
    for index in range(1, 16):
        total = total + parts_ref[index]
    for index in range(16):
        out_ref[index] = total


def diagonal(start_row, start_column, shape):
    rows = start_row + lax.broadcasted_iota(jnp.int32, shape, 0)
    columns = start_column + lax.broadcasted_iota(jnp.int32, shape, 1)
    return rows == columns


def final_kernel(mine_ref, other_ref, rows_ref, weight_ref, new_momentum_ref, new_weight_ref, residual_ref, gram_ref, first_ref, next_ref):
    near, far, core = place()
    tensor = lax.axis_index("tensor")
    spot = near * 64 + far * 16
    new_momentum_ref[...] = rows_ref[core, pl.ds(pl.multiple_of(spot, 16), 16)]
    for which in range(2):
        pick = core == which
        block = lambda start, size: jnp.where(pick, mine_ref[start : start + size], other_ref[start : start + size])
        base = 256 * which
        corner = block(128, 128)
        gram_ref[base : base + 128, base : base + 128] = block(0, 128)
        gram_ref[base : base + 128, base + 128 : base + 256] = corner
        gram_ref[base + 128 : base + 256, base : base + 128] = corner.T
        gram_ref[base + 128 : base + 256, base + 128 : base + 256] = block(256, 128)
        cross = block(384, 256)
        start = 256 + 128 * which
        gram_ref[0:256, start : start + 128] = cross
        gram_ref[start : start + 128, 0:256] = cross.T
    unit = diagonal(0, 0, (IN, IN))
    whole = gram_ref[...]
    squares = jnp.sum(jnp.sum(jnp.where(unit, whole, 0.0), axis=1, keepdims=True), axis=0, keepdims=True)
    inverse = 1.0 / (jnp.sqrt(squares) + epsilon)
    gram = (whole * inverse) * inverse
    pair = halves(gram)
    first = quintic_b * gram + quintic_c * mul3(pair, pair, NN) + jnp.where(unit, f32(quintic_a), f32(0.0))
    first_ref[...] = first
    first_pair = halves(first)
    inner = mul3(first_pair, pair, NN)
    after = mul3(first_pair, halves(inner), NN)
    next_ref[...] = after
    after_pair = halves(after)
    starts = [core * 256 + spot]
    for which in range(2):
        column = lax.rem(tensor + 16 - 2 * which, 16)
        starts.append(256 * which + lax.rem(column, 4) * 64 + lax.div(column, 4) * 16)
    bands = [next_ref[pl.ds(pl.multiple_of(start, 16), 16)] for start in starts]
    slab = jnp.concatenate(bands, axis=0)
    units = jnp.concatenate([diagonal(start, 0, (16, IN)) for start in starts], axis=0)
    second = quintic_b * slab + quintic_c * mul3(halves(slab), after_pair, NN) + jnp.where(units, f32(quintic_a), f32(0.0))
    own = halves(second[0:16])
    total = mul3(own, first_pair, NN)
    rows = rows_ref[...].reshape(IN, 256)
    update = mul3(halves(total), halves(rows), NN) * inverse
    scale = learn_rate * 0.2 * float(max(IN, OUT)) ** 0.5
    new_weight_ref[...] = weight_ref[...] * (1.0 - learn_rate * weight_decay) - scale * update
    product = mul3(own, after_pair, NN)
    final = mul3(halves(product), halves(second[16:48]), NT)
    identity = diagonal(lax.axis_index("dp") * 16, tensor * 32, (16, 32))
    residual_ref[...] = final - jnp.where(identity, f32(1.0), f32(0.0))


def call(kernel, outs, scratch=(), limit=4 << 20):
    return pl.pallas_call(
        kernel,
        out_shape=tuple(jax.ShapeDtypeStruct(shape, f32) for shape in outs),
        scratch_shapes=list(scratch),
        compiler_params=pltpu.CompilerParams(vmem_limit_bytes=limit),
    )


def exchange(value, axis, groups=None):
    return lax.all_to_all(value, axis, 0, 0, tiled=True, axis_index_groups=groups)


def per_device(gradients, momentum, weight):
    chunks = (4, 4, 16, 256)
    gradients = gradients.reshape(16, 2, 16, 256)
    (send,) = call(send_kernel, [chunks])(gradients)
    (parts,) = call(core_sum_kernel, [chunks])(gradients, lax.ppermute(send, "dp", CORE))
    (spread,) = call(near_sum_kernel, [chunks])(exchange(parts, "dp", NEAR), momentum)
    (spread,) = call(far_sum_kernel, [chunks])(exchange(spread, "dp", FAR))
    mine = exchange(spread, "dp", NEAR).reshape(256, 256)
    other = lax.ppermute(mine, "dp", CORE)
    blocks, rows = call(gram_kernel, [(640, 128), (2, 256, 256)], limit=8 << 20)(mine, other)
    (spread,) = call(tensor_sum_kernel, [(16, 40, 128)])(exchange(blocks.reshape(16, 40, 128), "tensor"))
    mine = exchange(spread, "tensor").reshape(640, 128)
    other = lax.ppermute(mine, "dp", CORE)
    return call(
        final_kernel,
        [(16, 256), (16, 256), (16, 32)],
        [pltpu.VMEM((IN, IN), f32)] * 3,
        limit=24 << 20,
    )(mine, other, rows, weight)


def solution(mesh):
    return jax.shard_map(
        per_device,
        mesh=mesh,
        in_specs=(P("dp", None, "tensor"), P("dp", "tensor"), P("dp", "tensor")),
        out_specs=(P("dp", "tensor"), P("dp", "tensor"), P("dp", "tensor")),
        check_vma=False,
    )
```

```python
import jax
import jax.numpy as jnp
from jax import lax
from jax.experimental import pallas as pl
from jax.experimental.pallas import tpu as pltpu
from jax.sharding import PartitionSpec as P

IN = 512
OUT = 4096

decay_rate = 0.95
learn_rate = 0.02
weight_decay = 0.1
epsilon = 1e-07
quintic_a = 3.4445
quintic_b = -4.775
quintic_c = 2.0315

f32 = jnp.float32
bf16 = jnp.bfloat16

CORE = [(i, i ^ 1) for i in range(32)]
NEAR = [[8 * far + 2 * near + core for near in range(4)] for far in range(4) for core in range(2)]
FAR = [[(i, i ^ (8 * step)) for i in range(32)] for step in (1, 2, 3)]

NT = (((1,), (1,)), ((), ()))
NN = (((1,), (0,)), ((), ()))


def place():
    index = lax.axis_index("dp")
    return lax.rem(lax.div(index, 2), 4), lax.div(index, 8), lax.rem(index, 2)


def halves(value):
    high = value.astype(bf16)
    low = (value - high.astype(f32)).astype(bf16)
    return high, low


def mul3(left, right, dims):
    dot = lambda x, y: lax.dot_general(x, y, dims, preferred_element_type=f32)
    return dot(left[0], right[0]) + (dot(left[0], right[1]) + dot(left[1], right[0]))


def send_kernel(grad_ref, send_ref):
    _, _, core = place()
    for near in range(4):
        for far in range(4):
            send_ref[near, far] = grad_ref[far, near, 1 - core].astype(f32)


def core_sum_kernel(grad_ref, got_ref, out_ref):
    _, _, core = place()
    for near in range(4):
        for far in range(4):
            out_ref[near, far] = grad_ref[far, near, core].astype(f32) + got_ref[near, far]


def near_sum_kernel(parts_ref, momentum_ref, out_ref):
    _, mine, _ = place()
    for far in range(4):
        total = (parts_ref[0, far] + parts_ref[1, far]) + (parts_ref[2, far] + parts_ref[3, far])
        out_ref[far] = total + jnp.where(mine == far, f32(decay_rate), f32(0.0)) * momentum_ref[...]


def far_sum_kernel(own_ref, first_ref, second_ref, third_ref, out_ref):
    for far in range(4):
        total = (own_ref[far] + first_ref[far]) + (second_ref[far] + third_ref[far])
        for other in range(4):
            out_ref[other, far] = total


def gram_kernel(mine_ref, other_ref, out_ref, rows_ref):
    _, _, core = place()
    rows_ref[core] = mine_ref[...]
    rows_ref[1 - core] = other_ref[...]
    own = halves(mine_ref[...])
    upper = tuple(part[:128] for part in own)
    lower = tuple(part[128:] for part in own)
    out_ref[0:128] = mul3(upper, upper, NT)
    out_ref[128:256] = mul3(upper, lower, NT)
    out_ref[256:384] = mul3(lower, lower, NT)
    left = halves(rows_ref[0])
    right = halves(rows_ref[1, pl.ds(pl.multiple_of(core * 128, 128), 128)])
    out_ref[384:640] = mul3(left, right, NT)


def tensor_sum_kernel(parts_ref, out_ref):
    total = parts_ref[0]
    for index in range(1, 16):
        total = total + parts_ref[index]
    for index in range(16):
        out_ref[index] = total


def diagonal(start_row, start_column, shape):
    rows = start_row + lax.broadcasted_iota(jnp.int32, shape, 0)
    columns = start_column + lax.broadcasted_iota(jnp.int32, shape, 1)
    return rows == columns


def final_kernel(mine_ref, other_ref, rows_ref, weight_ref, new_momentum_ref, new_weight_ref, residual_ref, gram_ref, first_ref, next_ref):
    near, far, core = place()
    tensor = lax.axis_index("tensor")
    spot = near * 64 + far * 16
    new_momentum_ref[...] = rows_ref[core, pl.ds(pl.multiple_of(spot, 16), 16)]
    for which in range(2):
        pick = core == which
        block = lambda start, size: jnp.where(pick, mine_ref[start : start + size], other_ref[start : start + size])
        base = 256 * which
        corner = block(128, 128)
        gram_ref[base : base + 128, base : base + 128] = block(0, 128)
        gram_ref[base : base + 128, base + 128 : base + 256] = corner
        gram_ref[base + 128 : base + 256, base : base + 128] = corner.T
        gram_ref[base + 128 : base + 256, base + 128 : base + 256] = block(256, 128)
        cross = block(384, 256)
        start = 256 + 128 * which
        gram_ref[0:256, start : start + 128] = cross
        gram_ref[start : start + 128, 0:256] = cross.T
    unit = diagonal(0, 0, (IN, IN))
    whole = gram_ref[...]
    squares = jnp.sum(jnp.sum(jnp.where(unit, whole, 0.0), axis=1, keepdims=True), axis=0, keepdims=True)
    inverse = 1.0 / (jnp.sqrt(squares) + epsilon)
    gram = (whole * inverse) * inverse
    pair = halves(gram)
    first = quintic_b * gram + quintic_c * mul3(pair, pair, NN) + jnp.where(unit, f32(quintic_a), f32(0.0))
    first_ref[...] = first
    first_pair = halves(first)
    inner = mul3(first_pair, pair, NN)
    after = mul3(first_pair, halves(inner), NN)
    next_ref[...] = after
    after_pair = halves(after)
    starts = [core * 256 + spot]
    for which in range(2):
        starts.append(256 * which + lax.rem(tensor, 4) * 64 + lax.div(tensor, 4) * 16)
    bands = [next_ref[pl.ds(pl.multiple_of(start, 16), 16)] for start in starts]
    slab = jnp.concatenate(bands, axis=0)
    units = jnp.concatenate([diagonal(start, 0, (16, IN)) for start in starts], axis=0)
    second = quintic_b * slab + quintic_c * mul3(halves(slab), after_pair, NN) + jnp.where(units, f32(quintic_a), f32(0.0))
    own = halves(second[0:16])
    total = mul3(own, first_pair, NN)
    rows = rows_ref[...].reshape(IN, 256)
    update = mul3(halves(total), halves(rows), NN) * inverse
    scale = learn_rate * 0.2 * float(max(IN, OUT)) ** 0.5
    new_weight_ref[...] = weight_ref[...] * (1.0 - learn_rate * weight_decay) - scale * update
    product = mul3(own, after_pair, NN)
    final = mul3(halves(product), halves(second[16:48]), NT)
    identity = diagonal(lax.axis_index("dp") * 16, tensor * 32, (16, 32))
    residual_ref[...] = final - jnp.where(identity, f32(1.0), f32(0.0))


def call(kernel, outs, scratch=(), limit=4 << 20):
    return pl.pallas_call(
        kernel,
        out_shape=tuple(jax.ShapeDtypeStruct(shape, f32) for shape in outs),
        scratch_shapes=list(scratch),
        compiler_params=pltpu.CompilerParams(vmem_limit_bytes=limit),
    )


def exchange(value, axis, groups=None):
    return lax.all_to_all(value, axis, 0, 0, tiled=True, axis_index_groups=groups)


def per_device(gradients, momentum, weight):
    chunks = (4, 4, 16, 256)
    gradients = gradients.reshape(4, 4, 2, 16, 256)
    (send,) = call(send_kernel, [chunks])(gradients)
    (parts,) = call(core_sum_kernel, [chunks])(gradients, lax.ppermute(send, "dp", CORE))
    (parts,) = call(near_sum_kernel, [chunks[1:]])(exchange(parts, "dp", NEAR), momentum)
    others = [lax.ppermute(parts, "dp", pairs) for pairs in FAR]
    (spread,) = call(far_sum_kernel, [chunks])(parts, *others)
    mine = exchange(spread, "dp", NEAR).reshape(256, 256)
    other = lax.ppermute(mine, "dp", CORE)
    blocks, rows = call(gram_kernel, [(640, 128), (2, 256, 256)], limit=8 << 20)(mine, other)
    (spread,) = call(tensor_sum_kernel, [(16, 40, 128)])(exchange(blocks.reshape(16, 40, 128), "tensor"))
    mine = exchange(spread, "tensor").reshape(640, 128)
    other = lax.ppermute(mine, "dp", CORE)
    return call(
        final_kernel,
        [(16, 256), (16, 256), (16, 32)],
        [pltpu.VMEM((IN, IN), f32)] * 3,
        limit=24 << 20,
    )(mine, other, rows, weight)


def solution(mesh):
    return jax.shard_map(
        per_device,
        mesh=mesh,
        in_specs=(P("dp", None, "tensor"), P("dp", "tensor"), P("dp", "tensor")),
        out_specs=(P("dp", "tensor"), P("dp", "tensor"), P("dp", "tensor")),
        check_vma=False,
    )
```

```python
import jax
import jax.numpy as jnp
from jax import lax
from jax.experimental import pallas as pl
from jax.experimental.pallas import tpu as pltpu
from jax.sharding import PartitionSpec as P

IN = 512
OUT = 4096

decay_rate = 0.95
learn_rate = 0.02
weight_decay = 0.1
epsilon = 1e-07
quintic_a = 3.4445
quintic_b = -4.775
quintic_c = 2.0315

f32 = jnp.float32
bf16 = jnp.bfloat16

CORE = [(i, i ^ 1) for i in range(32)]
NEAR = [[8 * far + 2 * near + core for near in range(4)] for far in range(4) for core in range(2)]
FAR = [[(i, i ^ (8 * step)) for i in range(32)] for step in (1, 3, 2)]

NT = (((1,), (1,)), ((), ()))
NN = (((1,), (0,)), ((), ()))


def place():
    index = lax.axis_index("dp")
    return lax.rem(lax.div(index, 2), 4), lax.div(index, 8), lax.rem(index, 2)


def halves(value):
    high = value.astype(bf16)
    low = (value - high.astype(f32)).astype(bf16)
    return high, low


def mul3(left, right, dims):
    dot = lambda x, y: lax.dot_general(x, y, dims, preferred_element_type=f32)
    return dot(left[0], right[0]) + (dot(left[0], right[1]) + dot(left[1], right[0]))


def send_kernel(grad_ref, send_ref):
    _, _, core = place()
    for near in range(4):
        for far in range(4):
            send_ref[near, far] = grad_ref[far, near, 1 - core].astype(f32)


def core_sum_kernel(grad_ref, got_ref, out_ref):
    _, _, core = place()
    for near in range(4):
        for far in range(4):
            out_ref[near, far] = grad_ref[far, near, core].astype(f32) + got_ref[near, far]


def near_sum_kernel(parts_ref, momentum_ref, out_ref):
    _, mine, _ = place()
    for far in range(4):
        total = (parts_ref[0, far] + parts_ref[1, far]) + (parts_ref[2, far] + parts_ref[3, far])
        out_ref[far] = total + jnp.where(mine == far, f32(decay_rate), f32(0.0)) * momentum_ref[...]


def far_sum_kernel(own_ref, first_ref, third_ref, second_ref, out_ref):
    for far in range(4):
        total = (own_ref[far] + first_ref[far]) + (second_ref[far] + third_ref[far])
        for other in range(4):
            out_ref[other, far] = total


def gram_kernel(mine_ref, other_ref, out_ref, rows_ref):
    _, _, core = place()
    rows_ref[core] = mine_ref[...]
    rows_ref[1 - core] = other_ref[...]
    own = halves(mine_ref[...])
    upper = tuple(part[:128] for part in own)
    lower = tuple(part[128:] for part in own)
    out_ref[0:128] = mul3(upper, upper, NT)
    out_ref[128:256] = mul3(upper, lower, NT)
    out_ref[256:384] = mul3(lower, lower, NT)
    left = halves(rows_ref[0])
    right = halves(rows_ref[1, pl.ds(pl.multiple_of(core * 128, 128), 128)])
    out_ref[384:640] = mul3(left, right, NT)


def tensor_sum_kernel(parts_ref, out_ref):
    total = parts_ref[0]
    for index in range(1, 16):
        total = total + parts_ref[index]
    for index in range(16):
        out_ref[index] = total


def diagonal(start_row, start_column, shape):
    rows = start_row + lax.broadcasted_iota(jnp.int32, shape, 0)
    columns = start_column + lax.broadcasted_iota(jnp.int32, shape, 1)
    return rows == columns


def final_kernel(mine_ref, other_ref, rows_ref, weight_ref, new_momentum_ref, new_weight_ref, residual_ref, gram_ref, first_ref, next_ref):
    near, far, core = place()
    tensor = lax.axis_index("tensor")
    spot = near * 64 + far * 16
    new_momentum_ref[...] = rows_ref[core, pl.ds(pl.multiple_of(spot, 16), 16)]
    for which in range(2):
        pick = core == which
        block = lambda start, size: jnp.where(pick, mine_ref[start : start + size], other_ref[start : start + size])
        base = 256 * which
        corner = block(128, 128)
        gram_ref[base : base + 128, base : base + 128] = block(0, 128)
        gram_ref[base : base + 128, base + 128 : base + 256] = corner
        gram_ref[base + 128 : base + 256, base : base + 128] = corner.T
        gram_ref[base + 128 : base + 256, base + 128 : base + 256] = block(256, 128)
        cross = block(384, 256)
        start = 256 + 128 * which
        gram_ref[0:256, start : start + 128] = cross
        gram_ref[start : start + 128, 0:256] = cross.T
    unit = diagonal(0, 0, (IN, IN))
    whole = gram_ref[...]
    squares = jnp.sum(jnp.sum(jnp.where(unit, whole, 0.0), axis=1, keepdims=True), axis=0, keepdims=True)
    inverse = 1.0 / (jnp.sqrt(squares) + epsilon)
    gram = (whole * inverse) * inverse
    pair = halves(gram)
    first = quintic_b * gram + quintic_c * mul3(pair, pair, NN) + jnp.where(unit, f32(quintic_a), f32(0.0))
    first_ref[...] = first
    first_pair = halves(first)
    inner = mul3(first_pair, pair, NN)
    after = mul3(first_pair, halves(inner), NN)
    next_ref[...] = after
    after_pair = halves(after)
    starts = [core * 256 + spot]
    for which in range(2):
        starts.append(256 * which + lax.rem(tensor, 4) * 64 + lax.div(tensor, 4) * 16)
    bands = [next_ref[pl.ds(pl.multiple_of(start, 16), 16)] for start in starts]
    slab = jnp.concatenate(bands, axis=0)
    units = jnp.concatenate([diagonal(start, 0, (16, IN)) for start in starts], axis=0)
    second = quintic_b * slab + quintic_c * mul3(halves(slab), after_pair, NN) + jnp.where(units, f32(quintic_a), f32(0.0))
    own = halves(second[0:16])
    total = mul3(own, first_pair, NN)
    rows = rows_ref[...].reshape(IN, 256)
    update = mul3(halves(total), halves(rows), NN) * inverse
    scale = learn_rate * 0.2 * float(max(IN, OUT)) ** 0.5
    new_weight_ref[...] = weight_ref[...] * (1.0 - learn_rate * weight_decay) - scale * update
    product = mul3(own, after_pair, NN)
    final = mul3(halves(product), halves(second[16:48]), NT)
    identity = diagonal(lax.axis_index("dp") * 16, tensor * 32, (16, 32))
    residual_ref[...] = final - jnp.where(identity, f32(1.0), f32(0.0))


def call(kernel, outs, scratch=(), limit=4 << 20):
    return pl.pallas_call(
        kernel,
        out_shape=tuple(jax.ShapeDtypeStruct(shape, f32) for shape in outs),
        scratch_shapes=list(scratch),
        compiler_params=pltpu.CompilerParams(vmem_limit_bytes=limit),
    )


def exchange(value, axis, groups=None):
    return lax.all_to_all(value, axis, 0, 0, tiled=True, axis_index_groups=groups)


def per_device(gradients, momentum, weight):
    chunks = (4, 4, 16, 256)
    gradients = gradients.reshape(4, 4, 2, 16, 256)
    (send,) = call(send_kernel, [chunks])(gradients)
    (parts,) = call(core_sum_kernel, [chunks])(gradients, lax.ppermute(send, "dp", CORE))
    (parts,) = call(near_sum_kernel, [chunks[1:]])(exchange(parts, "dp", NEAR), momentum)
    others = [lax.ppermute(parts, "dp", pairs) for pairs in FAR]
    (spread,) = call(far_sum_kernel, [chunks])(parts, *others)
    mine = exchange(spread, "dp", NEAR).reshape(256, 256)
    other = lax.ppermute(mine, "dp", CORE)
    blocks, rows = call(gram_kernel, [(640, 128), (2, 256, 256)], limit=8 << 20)(mine, other)
    (spread,) = call(tensor_sum_kernel, [(16, 40, 128)])(exchange(blocks.reshape(16, 40, 128), "tensor"))
    mine = exchange(spread, "tensor").reshape(640, 128)
    other = lax.ppermute(mine, "dp", CORE)
    return call(
        final_kernel,
        [(16, 256), (16, 256), (16, 32)],
        [pltpu.VMEM((IN, IN), f32)] * 3,
        limit=24 << 20,
    )(mine, other, rows, weight)


def solution(mesh):
    return jax.shard_map(
        per_device,
        mesh=mesh,
        in_specs=(P("dp", None, "tensor"), P("dp", "tensor"), P("dp", "tensor")),
        out_specs=(P("dp", "tensor"), P("dp", "tensor"), P("dp", "tensor")),
        check_vma=False,
    )
```

```python
import jax
import jax.numpy as jnp
from jax import lax
from jax.experimental import pallas as pl
from jax.experimental.pallas import tpu as pltpu
from jax.sharding import PartitionSpec as P

IN = 512
OUT = 4096

decay_rate = 0.95
learn_rate = 0.02
weight_decay = 0.1
epsilon = 1e-07
quintic_a = 3.4445
quintic_b = -4.775
quintic_c = 2.0315

f32 = jnp.float32
bf16 = jnp.bfloat16

CORE = [(i, i ^ 1) for i in range(32)]
NEAR = [[(i, i ^ (2 * step)) for i in range(32)] for step in (1, 2, 3)]
FAR = [[(i, i ^ (8 * step)) for i in range(32)] for step in (1, 3, 2)]

NT = (((1,), (1,)), ((), ()))
NN = (((1,), (0,)), ((), ()))


def place():
    index = lax.axis_index("dp")
    return lax.rem(lax.div(index, 2), 4), lax.div(index, 8), lax.rem(index, 2)


def halves(value):
    high = value.astype(bf16)
    low = (value - high.astype(f32)).astype(bf16)
    return high, low


def mul3(left, right, dims):
    dot = lambda x, y: lax.dot_general(x, y, dims, preferred_element_type=f32)
    return dot(left[0], right[0]) + (dot(left[0], right[1]) + dot(left[1], right[0]))


def send_kernel(grad_ref, send_ref):
    _, _, core = place()
    for near in range(4):
        for far in range(4):
            send_ref[near, far] = grad_ref[far, near, 1 - core].astype(f32)


def core_sum_kernel(grad_ref, got_ref, *out_refs):
    near, _, core = place()
    for step in range(4):
        other = near ^ step
        for far in range(4):
            out_refs[step][far] = grad_ref[far, other, core].astype(f32) + got_ref[other, far]


def near_sum_kernel(own_ref, first_ref, second_ref, third_ref, momentum_ref, out_ref):
    _, mine, _ = place()
    for far in range(4):
        total = (own_ref[far] + first_ref[far]) + (second_ref[far] + third_ref[far])
        out_ref[far] = total + jnp.where(mine == far, f32(decay_rate), f32(0.0)) * momentum_ref[...]


def far_sum_kernel(own_ref, first_ref, third_ref, second_ref, out_ref):
    for far in range(4):
        out_ref[far] = (own_ref[far] + first_ref[far]) + (second_ref[far] + third_ref[far])


def near_join_kernel(own_ref, first_ref, second_ref, third_ref, out_ref):
    near, _, _ = place()
    for step, part_ref in enumerate((own_ref, first_ref, second_ref, third_ref)):
        out_ref[near ^ step] = part_ref[...]


def gram_kernel(mine_ref, other_ref, out_ref, rows_ref):
    _, _, core = place()
    rows_ref[core] = mine_ref[...]
    rows_ref[1 - core] = other_ref[...]
    own = halves(mine_ref[...])
    upper = tuple(part[:128] for part in own)
    lower = tuple(part[128:] for part in own)
    out_ref[0:128] = mul3(upper, upper, NT)
    out_ref[128:256] = mul3(upper, lower, NT)
    out_ref[256:384] = mul3(lower, lower, NT)
    left = halves(rows_ref[0])
    right = halves(rows_ref[1, pl.ds(pl.multiple_of(core * 128, 128), 128)])
    out_ref[384:640] = mul3(left, right, NT)


def tensor_sum_kernel(parts_ref, out_ref):
    total = parts_ref[0]
    for index in range(1, 16):
        total = total + parts_ref[index]
    for index in range(16):
        out_ref[index] = total


def diagonal(start_row, start_column, shape):
    rows = start_row + lax.broadcasted_iota(jnp.int32, shape, 0)
    columns = start_column + lax.broadcasted_iota(jnp.int32, shape, 1)
    return rows == columns


def final_kernel(mine_ref, other_ref, rows_ref, weight_ref, new_momentum_ref, new_weight_ref, residual_ref, gram_ref, first_ref, next_ref):
    near, far, core = place()
    tensor = lax.axis_index("tensor")
    spot = near * 64 + far * 16
    new_momentum_ref[...] = rows_ref[core, pl.ds(pl.multiple_of(spot, 16), 16)]
    for which in range(2):
        pick = core == which
        block = lambda start, size: jnp.where(pick, mine_ref[start : start + size], other_ref[start : start + size])
        base = 256 * which
        corner = block(128, 128)
        gram_ref[base : base + 128, base : base + 128] = block(0, 128)
        gram_ref[base : base + 128, base + 128 : base + 256] = corner
        gram_ref[base + 128 : base + 256, base : base + 128] = corner.T
        gram_ref[base + 128 : base + 256, base + 128 : base + 256] = block(256, 128)
        cross = block(384, 256)
        start = 256 + 128 * which
        gram_ref[0:256, start : start + 128] = cross
        gram_ref[start : start + 128, 0:256] = cross.T
    unit = diagonal(0, 0, (IN, IN))
    whole = gram_ref[...]
    squares = jnp.sum(jnp.sum(jnp.where(unit, whole, 0.0), axis=1, keepdims=True), axis=0, keepdims=True)
    inverse = 1.0 / (jnp.sqrt(squares) + epsilon)
    gram = (whole * inverse) * inverse
    pair = halves(gram)
    first = quintic_b * gram + quintic_c * mul3(pair, pair, NN) + jnp.where(unit, f32(quintic_a), f32(0.0))
    first_ref[...] = first
    first_pair = halves(first)
    inner = mul3(first_pair, pair, NN)
    after = mul3(first_pair, halves(inner), NN)
    next_ref[...] = after
    after_pair = halves(after)
    starts = [core * 256 + spot]
    for which in range(2):
        starts.append(256 * which + lax.rem(tensor, 4) * 64 + lax.div(tensor, 4) * 16)
    bands = [next_ref[pl.ds(pl.multiple_of(start, 16), 16)] for start in starts]
    slab = jnp.concatenate(bands, axis=0)
    units = jnp.concatenate([diagonal(start, 0, (16, IN)) for start in starts], axis=0)
    second = quintic_b * slab + quintic_c * mul3(halves(slab), after_pair, NN) + jnp.where(units, f32(quintic_a), f32(0.0))
    own = halves(second[0:16])
    total = mul3(own, first_pair, NN)
    rows = rows_ref[...].reshape(IN, 256)
    update = mul3(halves(total), halves(rows), NN) * inverse
    scale = learn_rate * 0.2 * float(max(IN, OUT)) ** 0.5
    new_weight_ref[...] = weight_ref[...] * (1.0 - learn_rate * weight_decay) - scale * update
    product = mul3(own, after_pair, NN)
    final = mul3(halves(product), halves(second[16:48]), NT)
    identity = diagonal(lax.axis_index("dp") * 16, tensor * 32, (16, 32))
    residual_ref[...] = final - jnp.where(identity, f32(1.0), f32(0.0))


def call(kernel, outs, scratch=(), limit=4 << 20):
    return pl.pallas_call(
        kernel,
        out_shape=tuple(jax.ShapeDtypeStruct(shape, f32) for shape in outs),
        scratch_shapes=list(scratch),
        compiler_params=pltpu.CompilerParams(vmem_limit_bytes=limit),
    )


def exchange(value):
    return lax.all_to_all(value, "tensor", 0, 0, tiled=True)


def per_device(gradients, momentum, weight):
    chunks = (4, 4, 16, 256)
    gradients = gradients.reshape(4, 4, 2, 16, 256)
    (send,) = call(send_kernel, [chunks])(gradients)
    piece = chunks[1:]
    parts = call(core_sum_kernel, [piece] * 4)(gradients, lax.ppermute(send, "dp", CORE))
    others = [lax.ppermute(part, "dp", pairs) for part, pairs in zip(parts[1:], NEAR)]
    (part,) = call(near_sum_kernel, [piece])(parts[0], *others, momentum)
    others = [lax.ppermute(part, "dp", pairs) for pairs in FAR]
    (part,) = call(far_sum_kernel, [piece])(part, *others)
    others = [lax.ppermute(part, "dp", pairs) for pairs in NEAR]
    (mine,) = call(near_join_kernel, [chunks])(part, *others)
    mine = mine.reshape(256, 256)
    other = lax.ppermute(mine, "dp", CORE)
    blocks, rows = call(gram_kernel, [(640, 128), (2, 256, 256)], limit=8 << 20)(mine, other)
    (spread,) = call(tensor_sum_kernel, [(16, 40, 128)])(exchange(blocks.reshape(16, 40, 128)))
    mine = exchange(spread).reshape(640, 128)
    other = lax.ppermute(mine, "dp", CORE)
    return call(
        final_kernel,
        [(16, 256), (16, 256), (16, 32)],
        [pltpu.VMEM((IN, IN), f32)] * 3,
        limit=24 << 20,
    )(mine, other, rows, weight)


def solution(mesh):
    return jax.shard_map(
        per_device,
        mesh=mesh,
        in_specs=(P("dp", None, "tensor"), P("dp", "tensor"), P("dp", "tensor")),
        out_specs=(P("dp", "tensor"), P("dp", "tensor"), P("dp", "tensor")),
        check_vma=False,
    )
```

```python
import functools

import jax
import jax.numpy as jnp
from jax import lax
from jax.experimental import pallas as pl
from jax.experimental.pallas import tpu as pltpu
from jax.sharding import PartitionSpec as P

IN = 512
OUT = 4096

decay_rate = 0.95
learn_rate = 0.02
weight_decay = 0.1
epsilon = 1e-07
quintic_a = 3.4445
quintic_b = -4.775
quintic_c = 2.0315

f32 = jnp.float32
bf16 = jnp.bfloat16

ROWS = (64, 64)
MOST = max(ROWS)
BLOCKS = (((0, 0), (0, 1), (1, 1)), ((0, 2), (0, 3), (1, 2), (1, 3), (2, 2), (2, 3), (3, 3)))
TALL = 128 * max(len(blocks) for blocks in BLOCKS)

CORE = [(i, i ^ 1) for i in range(32)]
NEAR = [[8 * far + 2 * near + core for near in range(4)] for far in range(4) for core in range(2)]
FAR = [[[(i, i ^ (8 * step)) for i in range(core, 32, 2)] for step in (1, 3, 2)] for core in range(2)]

NT = (((1,), (1,)), ((), ()))
NN = (((1,), (0,)), ((), ()))


def place():
    index = lax.axis_index("dp")
    return lax.rem(lax.div(index, 2), 4), lax.div(index, 8), lax.rem(index, 2)


def halves(value):
    high = value.astype(bf16)
    low = (value - high.astype(f32)).astype(bf16)
    return high, low


def mul3(left, right, dims):
    dot = lambda x, y: lax.dot_general(x, y, dims, preferred_element_type=f32)
    return dot(left[0], right[0]) + (dot(left[0], right[1]) + dot(left[1], right[0]))


def local_rows(grad_ref, momentum_ref, side):
    near, far, core = place()
    first, last = (0, ROWS[0]) if side == 0 else (ROWS[0], 128)
    for piece in range(4):
        for chunk in range(8):
            low, high = max(first, 16 * chunk), min(last, 16 * chunk + 16)
            if low >= high:
                continue
            own = (near == piece) & (far == chunk // 2) & (core == chunk % 2)
            value = grad_ref[chunk // 2, piece, chunk % 2].astype(f32)
            value = value + jnp.where(own, f32(decay_rate), f32(0.0)) * momentum_ref[...]
            yield piece, low - first, value[low - 16 * chunk : high - 16 * chunk]


def send_kernel(grad_ref, momentum_ref, send_ref):
    _, _, core = place()
    for side in range(2):

        @pl.when(core != side)
        def _():
            for piece, start, value in local_rows(grad_ref, momentum_ref, side):
                send_ref[piece, start : start + value.shape[0]] = value
            if ROWS[side] < MOST:
                send_ref[:, ROWS[side] :] = jnp.zeros((4, MOST - ROWS[side], 256), f32)


def core_sum_kernel(side, grad_ref, momentum_ref, got_ref, out_ref):
    for piece, start, value in local_rows(grad_ref, momentum_ref, side):
        stop = start + value.shape[0]
        out_ref[piece, start:stop] = value + got_ref[piece, start:stop]


def near_sum_kernel(parts_ref, out_ref):
    out_ref[...] = (parts_ref[0] + parts_ref[1]) + (parts_ref[2] + parts_ref[3])


def far_sum_kernel(own_ref, first_ref, third_ref, second_ref, out_ref):
    total = (own_ref[...] + first_ref[...]) + (second_ref[...] + third_ref[...])
    for other in range(4):
        out_ref[other] = total


def join_kernel(mine_ref, other_ref, rows_ref):
    _, _, core = place()
    for side in range(2):

        @pl.when(core == side)
        def _():
            pair = (mine_ref, other_ref) if side == 0 else (other_ref, mine_ref)
            for piece in range(4):
                rows_ref[128 * piece : 128 * piece + ROWS[0]] = pair[0][piece, : ROWS[0]]
                rows_ref[128 * piece + ROWS[0] : 128 * piece + 128] = pair[1][piece, : ROWS[1]]


def gram_kernel(side, rows_ref, out_ref):
    pieces = {}
    for index, block in enumerate(BLOCKS[side]):
        for piece in block:
            if piece not in pieces:
                pieces[piece] = halves(rows_ref[128 * piece : 128 * piece + 128])
        out_ref[128 * index : 128 * index + 128] = mul3(pieces[block[0]], pieces[block[1]], NT)


def tensor_sum_kernel(parts_ref, out_ref):
    total = parts_ref[0]
    for index in range(1, 16):
        total = total + parts_ref[index]
    for index in range(16):
        out_ref[index] = total


def diagonal(start_row, start_column, shape):
    rows = start_row + lax.broadcasted_iota(jnp.int32, shape, 0)
    columns = start_column + lax.broadcasted_iota(jnp.int32, shape, 1)
    return rows == columns


def final_kernel(
    mine_ref, other_ref, rows_ref, weight_ref, new_momentum_ref, new_weight_ref, residual_ref,
    gram_ref, gram_high, gram_low, first_high, first_low, inner_high, inner_low, after_high, after_low,
):
    near, far, core = place()
    tensor = lax.axis_index("tensor")
    spot = pl.multiple_of(near * 128 + far * 32 + core * 16, 16)
    new_momentum_ref[...] = rows_ref[pl.ds(spot, 16)]
    trace = jnp.zeros((128, 128), f32)
    for side in range(2):
        for index, (row, column) in enumerate(BLOCKS[side]):
            start = 128 * index
            block = jnp.where(core == side, mine_ref[start : start + 128], other_ref[start : start + 128])
            gram_ref[128 * row : 128 * row + 128, 128 * column : 128 * column + 128] = block
            if row == column:
                trace = trace + block
            else:
                gram_ref[128 * column : 128 * column + 128, 128 * row : 128 * row + 128] = block.T
    trace = jnp.where(diagonal(0, 0, (128, 128)), trace, 0.0)
    squares = jnp.sum(jnp.sum(trace, axis=0, keepdims=True), axis=1, keepdims=True)
    inverse = 1.0 / (jnp.sqrt(squares) + epsilon)
    gram = (gram_ref[...] * inverse) * inverse
    gram_high[...], gram_low[...] = halves(gram)
    pair = (gram_high[...], gram_low[...])
    unit = jnp.where(diagonal(0, 0, (IN, IN)), f32(quintic_a), f32(0.0))
    first_high[...], first_low[...] = halves(quintic_b * gram + quintic_c * mul3(pair, pair, NN) + unit)
    first_pair = (first_high[...], first_low[...])
    inner_high[...], inner_low[...] = halves(mul3(first_pair, pair, NN))
    after_high[...], after_low[...] = halves(mul3(first_pair, (inner_high[...], inner_low[...]), NN))
    after_pair = (after_high[...], after_low[...])
    block_start = pl.multiple_of(lax.rem(tensor, 4) * 128 + lax.div(tensor, 4) * 32, 16)
    bands = ((spot, 16), (block_start, 32))
    slab = tuple(jnp.concatenate([part[pl.ds(*band)] for band in bands], axis=0) for part in (after_high, after_low))
    units = jnp.concatenate([diagonal(start, 0, (size, IN)) for start, size in bands], axis=0)
    second = quintic_b * (slab[0].astype(f32) + slab[1].astype(f32))
    second = second + quintic_c * mul3(slab, after_pair, NN) + jnp.where(units, f32(quintic_a), f32(0.0))
    second_pair = halves(second)
    own = tuple(part[0:16] for part in second_pair)
    total = mul3(own, first_pair, NN)
    update = mul3(halves(total), halves(rows_ref[...]), NN) * inverse
    scale = learn_rate * 0.2 * float(max(IN, OUT)) ** 0.5
    new_weight_ref[...] = weight_ref[...] * (1.0 - learn_rate * weight_decay) - scale * update
    product = mul3(own, after_pair, NN)
    final = mul3(halves(product), tuple(part[16:48] for part in second_pair), NT)
    identity = diagonal(lax.axis_index("dp") * 16, tensor * 32, (16, 32))
    residual_ref[...] = final - jnp.where(identity, f32(1.0), f32(0.0))


def call(kernel, outs, scratch=(), limit=4 << 20):
    return pl.pallas_call(
        kernel,
        out_shape=tuple(jax.ShapeDtypeStruct(shape, f32) for shape in outs),
        scratch_shapes=list(scratch),
        compiler_params=pltpu.CompilerParams(vmem_limit_bytes=limit),
    )


def exchange(value, axis, groups=None):
    return lax.all_to_all(value, axis, 0, 0, tiled=True, axis_index_groups=groups)


def pad(value, axis, size):
    widths = [(0, size - value.shape[axis] if index == axis else 0) for index in range(value.ndim)]
    return jnp.pad(value, widths)


def sum_replicas(side, gradients, momentum, got):
    parts, part = (4, ROWS[side], 256), (ROWS[side], 256)
    (value,) = call(functools.partial(core_sum_kernel, side), [parts])(gradients, momentum, got)
    (value,) = call(near_sum_kernel, [part])(exchange(value, "dp", NEAR))
    others = [lax.ppermute(value, "dp", pairs) for pairs in FAR[side]]
    (value,) = call(far_sum_kernel, [parts])(value, *others)
    return pad(exchange(value, "dp", NEAR), 1, MOST)


def sum_gram(side, rows):
    tall = 128 * len(BLOCKS[side])
    split = (16, tall // 16, 128)
    (blocks,) = call(functools.partial(gram_kernel, side), [(tall, 128)])(rows)
    (value,) = call(tensor_sum_kernel, [split])(exchange(blocks.reshape(split), "tensor"))
    return pad(exchange(value, "tensor").reshape(tall, 128), 0, TALL)


def per_core(function, *operands):
    first, second = (functools.partial(function, side) for side in range(2))
    return lax.cond(place()[2] == 0, first, second, *operands)


def per_device(gradients, momentum, weight):
    gradients = gradients.reshape(4, 4, 2, 16, 256)
    (send,) = call(send_kernel, [(4, MOST, 256)])(gradients, momentum)
    mine = per_core(sum_replicas, gradients, momentum, lax.ppermute(send, "dp", CORE))
    (rows,) = call(join_kernel, [(IN, 256)])(mine, lax.ppermute(mine, "dp", CORE))
    mine = per_core(sum_gram, rows)
    return call(
        final_kernel,
        [(16, 256), (16, 256), (16, 32)],
        [pltpu.VMEM((IN, IN), f32)] + [pltpu.VMEM((IN, IN), bf16)] * 8,
        limit=24 << 20,
    )(mine, lax.ppermute(mine, "dp", CORE), rows, weight)


def solution(mesh):
    return jax.shard_map(
        per_device,
        mesh=mesh,
        in_specs=(P("dp", None, "tensor"), P("dp", "tensor"), P("dp", "tensor")),
        out_specs=(P("dp", "tensor"), P("dp", "tensor"), P("dp", "tensor")),
        check_vma=False,
    )
```

```python
import functools

import jax
import jax.numpy as jnp
from jax import lax
from jax.experimental import pallas as pl
from jax.experimental.pallas import tpu as pltpu
from jax.sharding import PartitionSpec as P

IN = 512
OUT = 4096

decay_rate = 0.95
learn_rate = 0.02
weight_decay = 0.1
epsilon = 1e-07
quintic_a = 3.4445
quintic_b = -4.775
quintic_c = 2.0315

f32 = jnp.float32
bf16 = jnp.bfloat16

ROWS = (56, 72)
MOST = max(ROWS)
BLOCKS = (((0, 0), (0, 1), (0, 2), (0, 3), (1, 1)), ((1, 2), (1, 3), (2, 2), (2, 3), (3, 3)))
TALL = 128 * max(len(blocks) for blocks in BLOCKS)

CORE = [(i, i ^ 1) for i in range(32)]
NEAR = [[8 * far + 2 * near + core for near in range(4)] for far in range(4) for core in range(2)]
FAR = [[[(i, i ^ (8 * step)) for i in range(core, 32, 2)] for step in (1, 3, 2)] for core in range(2)]

NT = (((1,), (1,)), ((), ()))
NN = (((1,), (0,)), ((), ()))


def place():
    index = lax.axis_index("dp")
    return lax.rem(lax.div(index, 2), 4), lax.div(index, 8), lax.rem(index, 2)


def halves(value):
    high = value.astype(bf16)
    low = (value - high.astype(f32)).astype(bf16)
    return high, low


def mul3(left, right, dims):
    dot = lambda x, y: lax.dot_general(x, y, dims, preferred_element_type=f32)
    return dot(left[0], right[0]) + (dot(left[0], right[1]) + dot(left[1], right[0]))


def local_rows(grad_ref, momentum_ref, side):
    near, far, core = place()
    first, last = (0, ROWS[0]) if side == 0 else (ROWS[0], 128)
    for piece in range(4):
        for chunk in range(8):
            low, high = max(first, 16 * chunk), min(last, 16 * chunk + 16)
            if low >= high:
                continue
            own = (near == piece) & (far == chunk // 2) & (core == chunk % 2)
            value = grad_ref[chunk // 2, piece, chunk % 2].astype(f32)
            value = value + jnp.where(own, f32(decay_rate), f32(0.0)) * momentum_ref[...]
            yield piece, low - first, value[low - 16 * chunk : high - 16 * chunk]


def send_kernel(grad_ref, momentum_ref, send_ref):
    _, _, core = place()
    for side in range(2):

        @pl.when(core != side)
        def _():
            for piece, start, value in local_rows(grad_ref, momentum_ref, side):
                send_ref[piece, start : start + value.shape[0]] = value
            if ROWS[side] < MOST:
                send_ref[:, ROWS[side] :] = jnp.zeros((4, MOST - ROWS[side], 256), f32)


def core_sum_kernel(side, grad_ref, momentum_ref, got_ref, out_ref):
    for piece, start, value in local_rows(grad_ref, momentum_ref, side):
        stop = start + value.shape[0]
        out_ref[piece, start:stop] = value + got_ref[piece, start:stop]


def near_sum_kernel(parts_ref, out_ref):
    out_ref[...] = (parts_ref[0] + parts_ref[1]) + (parts_ref[2] + parts_ref[3])


def far_sum_kernel(own_ref, first_ref, third_ref, second_ref, out_ref):
    total = (own_ref[...] + first_ref[...]) + (second_ref[...] + third_ref[...])
    for other in range(4):
        out_ref[other] = total


def join_kernel(mine_ref, other_ref, rows_ref):
    _, _, core = place()
    for side in range(2):

        @pl.when(core == side)
        def _():
            pair = (mine_ref, other_ref) if side == 0 else (other_ref, mine_ref)
            for piece in range(4):
                rows_ref[128 * piece : 128 * piece + ROWS[0]] = pair[0][piece, : ROWS[0]]
                rows_ref[128 * piece + ROWS[0] : 128 * piece + 128] = pair[1][piece, : ROWS[1]]


def gram_kernel(side, rows_ref, out_ref):
    pieces = {}
    for index, block in enumerate(BLOCKS[side]):
        for piece in block:
            if piece not in pieces:
                pieces[piece] = halves(rows_ref[128 * piece : 128 * piece + 128])
        out_ref[128 * index : 128 * index + 128] = mul3(pieces[block[0]], pieces[block[1]], NT)


def tensor_sum_kernel(parts_ref, out_ref):
    total = parts_ref[0]
    for index in range(1, 16):
        total = total + parts_ref[index]
    for index in range(16):
        out_ref[index] = total


def diagonal(start_row, start_column, shape):
    rows = start_row + lax.broadcasted_iota(jnp.int32, shape, 0)
    columns = start_column + lax.broadcasted_iota(jnp.int32, shape, 1)
    return rows == columns


def final_kernel(
    mine_ref, other_ref, rows_ref, weight_ref, new_momentum_ref, new_weight_ref, residual_ref,
    gram_ref, gram_high, gram_low, first_high, first_low, inner_high, inner_low, after_high, after_low,
):
    near, far, core = place()
    tensor = lax.axis_index("tensor")
    spot = pl.multiple_of(near * 128 + far * 32 + core * 16, 16)
    new_momentum_ref[...] = rows_ref[pl.ds(spot, 16)]
    trace = jnp.zeros((128, 128), f32)
    for side in range(2):
        for index, (row, column) in enumerate(BLOCKS[side]):
            start = 128 * index
            block = jnp.where(core == side, mine_ref[start : start + 128], other_ref[start : start + 128])
            gram_ref[128 * row : 128 * row + 128, 128 * column : 128 * column + 128] = block
            if row == column:
                trace = trace + block
            else:
                gram_ref[128 * column : 128 * column + 128, 128 * row : 128 * row + 128] = block.T
    trace = jnp.where(diagonal(0, 0, (128, 128)), trace, 0.0)
    squares = jnp.sum(jnp.sum(trace, axis=0, keepdims=True), axis=1, keepdims=True)
    inverse = 1.0 / (jnp.sqrt(squares) + epsilon)
    gram = (gram_ref[...] * inverse) * inverse
    gram_high[...], gram_low[...] = halves(gram)
    pair = (gram_high[...], gram_low[...])
    unit = jnp.where(diagonal(0, 0, (IN, IN)), f32(quintic_a), f32(0.0))
    first_high[...], first_low[...] = halves(quintic_b * gram + quintic_c * mul3(pair, pair, NN) + unit)
    first_pair = (first_high[...], first_low[...])
    inner_high[...], inner_low[...] = halves(mul3(first_pair, pair, NN))
    after_high[...], after_low[...] = halves(mul3(first_pair, (inner_high[...], inner_low[...]), NN))
    after_pair = (after_high[...], after_low[...])
    block_start = pl.multiple_of(lax.rem(tensor, 4) * 128 + lax.div(tensor, 4) * 32, 16)
    bands = ((spot, 16), (block_start, 32))
    slab = tuple(jnp.concatenate([part[pl.ds(*band)] for band in bands], axis=0) for part in (after_high, after_low))
    units = jnp.concatenate([diagonal(start, 0, (size, IN)) for start, size in bands], axis=0)
    second = quintic_b * (slab[0].astype(f32) + slab[1].astype(f32))
    second = second + quintic_c * mul3(slab, after_pair, NN) + jnp.where(units, f32(quintic_a), f32(0.0))
    second_pair = halves(second)
    own = tuple(part[0:16] for part in second_pair)
    total = mul3(own, first_pair, NN)
    update = mul3(halves(total), halves(rows_ref[...]), NN) * inverse
    scale = learn_rate * 0.2 * float(max(IN, OUT)) ** 0.5
    new_weight_ref[...] = weight_ref[...] * (1.0 - learn_rate * weight_decay) - scale * update
    product = mul3(own, after_pair, NN)
    final = mul3(halves(product), tuple(part[16:48] for part in second_pair), NT)
    identity = diagonal(lax.axis_index("dp") * 16, tensor * 32, (16, 32))
    residual_ref[...] = final - jnp.where(identity, f32(1.0), f32(0.0))


def call(kernel, outs, scratch=(), limit=4 << 20):
    return pl.pallas_call(
        kernel,
        out_shape=tuple(jax.ShapeDtypeStruct(shape, f32) for shape in outs),
        scratch_shapes=list(scratch),
        compiler_params=pltpu.CompilerParams(vmem_limit_bytes=limit),
    )


def exchange(value, axis, groups=None):
    return lax.all_to_all(value, axis, 0, 0, tiled=True, axis_index_groups=groups)


def pad(value, axis, size):
    widths = [(0, size - value.shape[axis] if index == axis else 0) for index in range(value.ndim)]
    return jnp.pad(value, widths)


def sum_replicas(side, gradients, momentum, got):
    parts, part = (4, ROWS[side], 256), (ROWS[side], 256)
    (value,) = call(functools.partial(core_sum_kernel, side), [parts])(gradients, momentum, got)
    (value,) = call(near_sum_kernel, [part])(exchange(value, "dp", NEAR))
    others = [lax.ppermute(value, "dp", pairs) for pairs in FAR[side]]
    (value,) = call(far_sum_kernel, [parts])(value, *others)
    return pad(exchange(value, "dp", NEAR), 1, MOST)


def sum_gram(side, rows):
    tall = 128 * len(BLOCKS[side])
    split = (16, tall // 16, 128)
    (blocks,) = call(functools.partial(gram_kernel, side), [(tall, 128)])(rows)
    (value,) = call(tensor_sum_kernel, [split])(exchange(blocks.reshape(split), "tensor"))
    return pad(exchange(value, "tensor").reshape(tall, 128), 0, TALL)


def per_core(function, *operands):
    first, second = (functools.partial(function, side) for side in range(2))
    return lax.cond(place()[2] == 0, first, second, *operands)


def per_device(gradients, momentum, weight):
    gradients = gradients.reshape(4, 4, 2, 16, 256)
    (send,) = call(send_kernel, [(4, MOST, 256)])(gradients, momentum)
    mine = per_core(sum_replicas, gradients, momentum, lax.ppermute(send, "dp", CORE))
    (rows,) = call(join_kernel, [(IN, 256)])(mine, lax.ppermute(mine, "dp", CORE))
    mine = per_core(sum_gram, rows)
    return call(
        final_kernel,
        [(16, 256), (16, 256), (16, 32)],
        [pltpu.VMEM((IN, IN), f32)] + [pltpu.VMEM((IN, IN), bf16)] * 8,
        limit=24 << 20,
    )(mine, lax.ppermute(mine, "dp", CORE), rows, weight)


def solution(mesh):
    return jax.shard_map(
        per_device,
        mesh=mesh,
        in_specs=(P("dp", None, "tensor"), P("dp", "tensor"), P("dp", "tensor")),
        out_specs=(P("dp", "tensor"), P("dp", "tensor"), P("dp", "tensor")),
        check_vma=False,
    )
```

```python
import jax
import jax.numpy as jnp
from jax import lax
from jax.experimental import pallas as pl
from jax.experimental.pallas import tpu as pltpu
from jax.sharding import PartitionSpec as P

IN = 512
OUT = 4096

decay_rate = 0.95
learn_rate = 0.02
weight_decay = 0.1
epsilon = 1e-07
quintic_a = 3.4445
quintic_b = -4.775
quintic_c = 2.0315

f32 = jnp.float32
bf16 = jnp.bfloat16

CORE = [(i, i ^ 1) for i in range(32)]
NEAR = [[8 * far + 2 * near + core for near in range(4)] for far in range(4) for core in range(2)]
FAR = [[(i, i ^ (8 * steps[i % 2])) for i in range(32)] for steps in ((1, 3), (3, 1), (2, 2))]

NT = (((1,), (1,)), ((), ()))
NN = (((1,), (0,)), ((), ()))


def place():
    index = lax.axis_index("dp")
    return lax.rem(lax.div(index, 2), 4), lax.div(index, 8), lax.rem(index, 2)


def halves(value):
    high = value.astype(bf16)
    low = (value - high.astype(f32)).astype(bf16)
    return high, low


def mul3(left, right, dims):
    dot = lambda x, y: lax.dot_general(x, y, dims, preferred_element_type=f32)
    return dot(left[0], right[0]) + (dot(left[0], right[1]) + dot(left[1], right[0]))


def send_kernel(grad_ref, send_ref):
    _, _, core = place()
    for near in range(4):
        for far in range(4):
            send_ref[near, far] = grad_ref[far, near, 1 - core].astype(f32)


def core_sum_kernel(grad_ref, got_ref, out_ref):
    _, _, core = place()
    for near in range(4):
        for far in range(4):
            out_ref[near, far] = grad_ref[far, near, core].astype(f32) + got_ref[near, far]


def near_sum_kernel(parts_ref, momentum_ref, out_ref):
    _, mine, _ = place()
    for far in range(4):
        total = (parts_ref[0, far] + parts_ref[1, far]) + (parts_ref[2, far] + parts_ref[3, far])
        out_ref[far] = total + jnp.where(mine == far, f32(decay_rate), f32(0.0)) * momentum_ref[...]


def far_sum_kernel(own_ref, last_ref, middle_ref, second_ref, out_ref):
    _, _, core = place()
    for far in range(4):
        first = jnp.where(core == 0, last_ref[far], middle_ref[far])
        third = jnp.where(core == 0, middle_ref[far], last_ref[far])
        total = (own_ref[far] + first) + (second_ref[far] + third)
        for other in range(4):
            out_ref[other, far] = total


def gram_kernel(mine_ref, other_ref, out_ref, rows_ref):
    _, _, core = place()
    rows_ref[core] = mine_ref[...]
    rows_ref[1 - core] = other_ref[...]
    own = halves(mine_ref[...])
    upper = tuple(part[:128] for part in own)
    lower = tuple(part[128:] for part in own)
    out_ref[0:128] = mul3(upper, upper, NT)
    out_ref[128:256] = mul3(upper, lower, NT)
    out_ref[256:384] = mul3(lower, lower, NT)
    left = halves(rows_ref[0])
    right = halves(rows_ref[1, pl.ds(pl.multiple_of(core * 128, 128), 128)])
    out_ref[384:640] = mul3(left, right, NT)


def tensor_sum_kernel(parts_ref, out_ref):
    total = parts_ref[0]
    for index in range(1, 16):
        total = total + parts_ref[index]
    for index in range(16):
        out_ref[index] = total


def diagonal(start_row, start_column, shape):
    rows = start_row + lax.broadcasted_iota(jnp.int32, shape, 0)
    columns = start_column + lax.broadcasted_iota(jnp.int32, shape, 1)
    return rows == columns


def final_kernel(mine_ref, other_ref, rows_ref, weight_ref, new_momentum_ref, new_weight_ref, residual_ref, gram_ref, first_ref, next_ref):
    near, far, core = place()
    tensor = lax.axis_index("tensor")
    spot = near * 64 + far * 16
    new_momentum_ref[...] = rows_ref[core, pl.ds(pl.multiple_of(spot, 16), 16)]
    for which in range(2):
        pick = core == which
        block = lambda start, size: jnp.where(pick, mine_ref[start : start + size], other_ref[start : start + size])
        base = 256 * which
        corner = block(128, 128)
        gram_ref[base : base + 128, base : base + 128] = block(0, 128)
        gram_ref[base : base + 128, base + 128 : base + 256] = corner
        gram_ref[base + 128 : base + 256, base : base + 128] = corner.T
        gram_ref[base + 128 : base + 256, base + 128 : base + 256] = block(256, 128)
        cross = block(384, 256)
        start = 256 + 128 * which
        gram_ref[0:256, start : start + 128] = cross
        gram_ref[start : start + 128, 0:256] = cross.T
    unit = diagonal(0, 0, (IN, IN))
    whole = gram_ref[...]
    squares = jnp.sum(jnp.sum(jnp.where(unit, whole, 0.0), axis=1, keepdims=True), axis=0, keepdims=True)
    inverse = 1.0 / (jnp.sqrt(squares) + epsilon)
    gram = (whole * inverse) * inverse
    pair = halves(gram)
    first = quintic_b * gram + quintic_c * mul3(pair, pair, NN) + jnp.where(unit, f32(quintic_a), f32(0.0))
    first_ref[...] = first
    first_pair = halves(first)
    inner = mul3(first_pair, pair, NN)
    after = mul3(first_pair, halves(inner), NN)
    next_ref[...] = after
    after_pair = halves(after)
    starts = [core * 256 + spot]
    for which in range(2):
        starts.append(256 * which + lax.rem(tensor, 4) * 64 + lax.div(tensor, 4) * 16)
    bands = [next_ref[pl.ds(pl.multiple_of(start, 16), 16)] for start in starts]
    slab = jnp.concatenate(bands, axis=0)
    units = jnp.concatenate([diagonal(start, 0, (16, IN)) for start in starts], axis=0)
    second = quintic_b * slab + quintic_c * mul3(halves(slab), after_pair, NN) + jnp.where(units, f32(quintic_a), f32(0.0))
    own = halves(second[0:16])
    total = mul3(own, first_pair, NN)
    rows = rows_ref[...].reshape(IN, 256)
    update = mul3(halves(total), halves(rows), NN) * inverse
    scale = learn_rate * 0.2 * float(max(IN, OUT)) ** 0.5
    new_weight_ref[...] = weight_ref[...] * (1.0 - learn_rate * weight_decay) - scale * update
    product = mul3(own, after_pair, NN)
    final = mul3(halves(product), halves(second[16:48]), NT)
    identity = diagonal(lax.axis_index("dp") * 16, tensor * 32, (16, 32))
    residual_ref[...] = final - jnp.where(identity, f32(1.0), f32(0.0))


def call(kernel, outs, scratch=(), limit=4 << 20):
    return pl.pallas_call(
        kernel,
        out_shape=tuple(jax.ShapeDtypeStruct(shape, f32) for shape in outs),
        scratch_shapes=list(scratch),
        compiler_params=pltpu.CompilerParams(vmem_limit_bytes=limit),
    )


def exchange(value, axis, groups=None):
    return lax.all_to_all(value, axis, 0, 0, tiled=True, axis_index_groups=groups)


def per_device(gradients, momentum, weight):
    chunks = (4, 4, 16, 256)
    gradients = gradients.reshape(4, 4, 2, 16, 256)
    (send,) = call(send_kernel, [chunks])(gradients)
    (parts,) = call(core_sum_kernel, [chunks])(gradients, lax.ppermute(send, "dp", CORE))
    (parts,) = call(near_sum_kernel, [chunks[1:]])(exchange(parts, "dp", NEAR), momentum)
    others = [lax.ppermute(parts, "dp", pairs) for pairs in FAR]
    (spread,) = call(far_sum_kernel, [chunks])(parts, *others)
    mine = exchange(spread, "dp", NEAR).reshape(256, 256)
    other = lax.ppermute(mine, "dp", CORE)
    blocks, rows = call(gram_kernel, [(640, 128), (2, 256, 256)], limit=8 << 20)(mine, other)
    (spread,) = call(tensor_sum_kernel, [(16, 40, 128)])(exchange(blocks.reshape(16, 40, 128), "tensor"))
    mine = exchange(spread, "tensor").reshape(640, 128)
    other = lax.ppermute(mine, "dp", CORE)
    return call(
        final_kernel,
        [(16, 256), (16, 256), (16, 32)],
        [pltpu.VMEM((IN, IN), f32)] * 3,
        limit=24 << 20,
    )(mine, other, rows, weight)


def solution(mesh):
    return jax.shard_map(
        per_device,
        mesh=mesh,
        in_specs=(P("dp", None, "tensor"), P("dp", "tensor"), P("dp", "tensor")),
        out_specs=(P("dp", "tensor"), P("dp", "tensor"), P("dp", "tensor")),
        check_vma=False,
    )
```

```python
import jax
import jax.numpy as jnp
from jax import lax
from jax.experimental import pallas as pl
from jax.experimental.pallas import tpu as pltpu
from jax.sharding import PartitionSpec as P

IN = 512
OUT = 4096

decay_rate = 0.95
learn_rate = 0.02
weight_decay = 0.1
epsilon = 1e-07
quintic_a = 3.4445
quintic_b = -4.775
quintic_c = 2.0315

f32 = jnp.float32
bf16 = jnp.bfloat16

CORE = [(i, i ^ 1) for i in range(32)]
NEAR = [[8 * far + 2 * near + core for near in range(4)] for far in range(4) for core in range(2)]
FAR = [[(i, i ^ (8 * steps[i % 2])) for i in range(32)] for steps in ((1, 3), (3, 1))]

NT = (((1,), (1,)), ((), ()))
NN = (((1,), (0,)), ((), ()))


def place():
    index = lax.axis_index("dp")
    return lax.rem(lax.div(index, 2), 4), lax.div(index, 8), lax.rem(index, 2)


def halves(value):
    high = value.astype(bf16)
    low = (value - high.astype(f32)).astype(bf16)
    return high, low


def mul3(left, right, dims):
    dot = lambda x, y: lax.dot_general(x, y, dims, preferred_element_type=f32)
    return dot(left[0], right[0]) + (dot(left[0], right[1]) + dot(left[1], right[0]))


def send_kernel(grad_ref, send_ref):
    _, _, core = place()
    for near in range(4):
        for far in range(4):
            send_ref[near, far] = grad_ref[far, near, 1 - core].astype(f32)


def core_sum_kernel(grad_ref, got_ref, out_ref):
    _, _, core = place()
    for near in range(4):
        for far in range(4):
            out_ref[near, far] = grad_ref[far, near, core].astype(f32) + got_ref[near, far]


def near_sum_kernel(parts_ref, momentum_ref, out_ref):
    _, mine, _ = place()
    for far in range(4):
        total = (parts_ref[0, far] + parts_ref[1, far]) + (parts_ref[2, far] + parts_ref[3, far])
        out_ref[far] = total + jnp.where(mine == far, f32(decay_rate), f32(0.0)) * momentum_ref[...]


def far_sum_kernel(own_ref, other_ref, out_ref):
    for far in range(4):
        total = own_ref[far] + other_ref[far]
        for other in range(4):
            out_ref[other, far] = total


def gram_kernel(mine_ref, other_ref, out_ref, rows_ref):
    _, _, core = place()
    rows_ref[core] = mine_ref[...]
    rows_ref[1 - core] = other_ref[...]
    own = halves(mine_ref[...])
    upper = tuple(part[:128] for part in own)
    lower = tuple(part[128:] for part in own)
    out_ref[0:128] = mul3(upper, upper, NT)
    out_ref[128:256] = mul3(upper, lower, NT)
    out_ref[256:384] = mul3(lower, lower, NT)
    left = halves(rows_ref[0])
    right = halves(rows_ref[1, pl.ds(pl.multiple_of(core * 128, 128), 128)])
    out_ref[384:640] = mul3(left, right, NT)


def tensor_sum_kernel(parts_ref, out_ref):
    total = parts_ref[0]
    for index in range(1, 16):
        total = total + parts_ref[index]
    for index in range(16):
        out_ref[index] = total


def diagonal(start_row, start_column, shape):
    rows = start_row + lax.broadcasted_iota(jnp.int32, shape, 0)
    columns = start_column + lax.broadcasted_iota(jnp.int32, shape, 1)
    return rows == columns


def final_kernel(mine_ref, other_ref, rows_ref, weight_ref, new_momentum_ref, new_weight_ref, residual_ref, gram_ref, first_ref, next_ref):
    near, far, core = place()
    tensor = lax.axis_index("tensor")
    spot = near * 64 + far * 16
    new_momentum_ref[...] = rows_ref[core, pl.ds(pl.multiple_of(spot, 16), 16)]
    for which in range(2):
        pick = core == which
        block = lambda start, size: jnp.where(pick, mine_ref[start : start + size], other_ref[start : start + size])
        base = 256 * which
        corner = block(128, 128)
        gram_ref[base : base + 128, base : base + 128] = block(0, 128)
        gram_ref[base : base + 128, base + 128 : base + 256] = corner
        gram_ref[base + 128 : base + 256, base : base + 128] = corner.T
        gram_ref[base + 128 : base + 256, base + 128 : base + 256] = block(256, 128)
        cross = block(384, 256)
        start = 256 + 128 * which
        gram_ref[0:256, start : start + 128] = cross
        gram_ref[start : start + 128, 0:256] = cross.T
    unit = diagonal(0, 0, (IN, IN))
    whole = gram_ref[...]
    squares = jnp.sum(jnp.sum(jnp.where(unit, whole, 0.0), axis=1, keepdims=True), axis=0, keepdims=True)
    inverse = 1.0 / (jnp.sqrt(squares) + epsilon)
    gram = (whole * inverse) * inverse
    pair = halves(gram)
    first = quintic_b * gram + quintic_c * mul3(pair, pair, NN) + jnp.where(unit, f32(quintic_a), f32(0.0))
    first_ref[...] = first
    first_pair = halves(first)
    inner = mul3(first_pair, pair, NN)
    after = mul3(first_pair, halves(inner), NN)
    next_ref[...] = after
    after_pair = halves(after)
    starts = [core * 256 + spot]
    for which in range(2):
        starts.append(256 * which + lax.rem(tensor, 4) * 64 + lax.div(tensor, 4) * 16)
    bands = [next_ref[pl.ds(pl.multiple_of(start, 16), 16)] for start in starts]
    slab = jnp.concatenate(bands, axis=0)
    units = jnp.concatenate([diagonal(start, 0, (16, IN)) for start in starts], axis=0)
    second = quintic_b * slab + quintic_c * mul3(halves(slab), after_pair, NN) + jnp.where(units, f32(quintic_a), f32(0.0))
    own = halves(second[0:16])
    total = mul3(own, first_pair, NN)
    rows = rows_ref[...].reshape(IN, 256)
    update = mul3(halves(total), halves(rows), NN) * inverse
    scale = learn_rate * 0.2 * float(max(IN, OUT)) ** 0.5
    new_weight_ref[...] = weight_ref[...] * (1.0 - learn_rate * weight_decay) - scale * update
    product = mul3(own, after_pair, NN)
    final = mul3(halves(product), halves(second[16:48]), NT)
    identity = diagonal(lax.axis_index("dp") * 16, tensor * 32, (16, 32))
    residual_ref[...] = final - jnp.where(identity, f32(1.0), f32(0.0))


def call(kernel, outs, scratch=(), limit=4 << 20):
    return pl.pallas_call(
        kernel,
        out_shape=tuple(jax.ShapeDtypeStruct(shape, f32) for shape in outs),
        scratch_shapes=list(scratch),
        compiler_params=pltpu.CompilerParams(vmem_limit_bytes=limit),
    )


def exchange(value, axis, groups=None):
    return lax.all_to_all(value, axis, 0, 0, tiled=True, axis_index_groups=groups)


def per_device(gradients, momentum, weight):
    chunks = (4, 4, 16, 256)
    gradients = gradients.reshape(4, 4, 2, 16, 256)
    (send,) = call(send_kernel, [chunks])(gradients)
    (parts,) = call(core_sum_kernel, [chunks])(gradients, lax.ppermute(send, "dp", CORE))
    (parts,) = call(near_sum_kernel, [chunks[1:]])(exchange(parts, "dp", NEAR), momentum)
    parts = parts + lax.ppermute(parts, "dp", FAR[0])
    (spread,) = call(far_sum_kernel, [chunks])(parts, lax.ppermute(parts, "dp", FAR[1]))
    mine = exchange(spread, "dp", NEAR).reshape(256, 256)
    other = lax.ppermute(mine, "dp", CORE)
    blocks, rows = call(gram_kernel, [(640, 128), (2, 256, 256)], limit=8 << 20)(mine, other)
    (spread,) = call(tensor_sum_kernel, [(16, 40, 128)])(exchange(blocks.reshape(16, 40, 128), "tensor"))
    mine = exchange(spread, "tensor").reshape(640, 128)
    other = lax.ppermute(mine, "dp", CORE)
    return call(
        final_kernel,
        [(16, 256), (16, 256), (16, 32)],
        [pltpu.VMEM((IN, IN), f32)] * 3,
        limit=24 << 20,
    )(mine, other, rows, weight)


def solution(mesh):
    return jax.shard_map(
        per_device,
        mesh=mesh,
        in_specs=(P("dp", None, "tensor"), P("dp", "tensor"), P("dp", "tensor")),
        out_specs=(P("dp", "tensor"), P("dp", "tensor"), P("dp", "tensor")),
        check_vma=False,
    )
```

```python
import jax
import jax.numpy as jnp
from jax import lax
from jax.experimental import pallas as pl
from jax.experimental.pallas import tpu as pltpu
from jax.sharding import PartitionSpec as P

IN = 512
OUT = 4096

decay_rate = 0.95
learn_rate = 0.02
weight_decay = 0.1
epsilon = 1e-07
quintic_a = 3.4445
quintic_b = -4.775
quintic_c = 2.0315

f32 = jnp.float32
bf16 = jnp.bfloat16

CORE = [(i, i ^ 1) for i in range(32)]
NEAR = [[8 * far + 2 * near + core for near in range(4)] for far in range(4) for core in range(2)]
FAR = [[(i, i ^ (8 * steps[(i + i // 4) % 2])) for i in range(32)] for steps in ((1, 3), (3, 1))]

NT = (((1,), (1,)), ((), ()))
NN = (((1,), (0,)), ((), ()))


def place():
    index = lax.axis_index("dp")
    return lax.rem(lax.div(index, 2), 4), lax.div(index, 8), lax.rem(index, 2)


def halves(value):
    high = value.astype(bf16)
    low = (value - high.astype(f32)).astype(bf16)
    return high, low


def mul3(left, right, dims):
    dot = lambda x, y: lax.dot_general(x, y, dims, preferred_element_type=f32)
    return dot(left[0], right[0]) + (dot(left[0], right[1]) + dot(left[1], right[0]))


def send_kernel(grad_ref, send_ref):
    _, _, core = place()
    for near in range(4):
        for far in range(4):
            send_ref[near, far] = grad_ref[far, near, 1 - core].astype(f32)


def core_sum_kernel(grad_ref, got_ref, out_ref):
    _, _, core = place()
    for near in range(4):
        for far in range(4):
            out_ref[near, far] = grad_ref[far, near, core].astype(f32) + got_ref[near, far]


def near_sum_kernel(parts_ref, momentum_ref, out_ref):
    _, mine, _ = place()
    for far in range(4):
        total = (parts_ref[0, far] + parts_ref[1, far]) + (parts_ref[2, far] + parts_ref[3, far])
        out_ref[far] = total + jnp.where(mine == far, f32(decay_rate), f32(0.0)) * momentum_ref[...]


def far_sum_kernel(own_ref, other_ref, out_ref):
    for far in range(4):
        total = own_ref[far] + other_ref[far]
        for other in range(4):
            out_ref[other, far] = total


def gram_kernel(mine_ref, other_ref, out_ref, rows_ref):
    _, _, core = place()
    rows_ref[core] = mine_ref[...]
    rows_ref[1 - core] = other_ref[...]
    own = halves(mine_ref[...])
    upper = tuple(part[:128] for part in own)
    lower = tuple(part[128:] for part in own)
    out_ref[0:128] = mul3(upper, upper, NT)
    out_ref[128:256] = mul3(upper, lower, NT)
    out_ref[256:384] = mul3(lower, lower, NT)
    left = halves(rows_ref[0])
    right = halves(rows_ref[1, pl.ds(pl.multiple_of(core * 128, 128), 128)])
    out_ref[384:640] = mul3(left, right, NT)


def tensor_sum_kernel(parts_ref, out_ref):
    total = parts_ref[0]
    for index in range(1, 16):
        total = total + parts_ref[index]
    for index in range(16):
        out_ref[index] = total


def diagonal(start_row, start_column, shape):
    rows = start_row + lax.broadcasted_iota(jnp.int32, shape, 0)
    columns = start_column + lax.broadcasted_iota(jnp.int32, shape, 1)
    return rows == columns


def multiply(left, right, out, change):
    top, low = slice(0, 256), slice(256, 512)
    pick = lambda pair, rows, columns: tuple(part[rows, columns] for part in pair)
    whole = slice(0, 512)
    upper = change(mul3(pick(left, top, whole), pick(right, whole, whole), NN), top, whole)
    lower = change(mul3(pick(left, low, whole), pick(right, whole, low), NN), low, low)
    out[0][top], out[1][top] = halves(upper)
    out[0][low, low], out[1][low, low] = halves(lower)
    out[0][low, top], out[1][low, top] = halves(upper[:, low].T)


def final_kernel(
    mine_ref, other_ref, rows_ref, weight_ref, new_momentum_ref, new_weight_ref, residual_ref,
    gram_ref, gram_high, gram_low, first_high, first_low, inner_high, inner_low, after_high, after_low,
):
    near, far, core = place()
    tensor = lax.axis_index("tensor")
    spot = near * 64 + far * 16
    new_momentum_ref[...] = rows_ref[core, pl.ds(pl.multiple_of(spot, 16), 16)]
    trace = jnp.zeros((128, 128), f32)
    for which in range(2):
        pick = core == which
        block = lambda start, size: jnp.where(pick, mine_ref[start : start + size], other_ref[start : start + size])
        base = 256 * which
        head, corner, tail = block(0, 128), block(128, 128), block(256, 128)
        trace = trace + head + tail
        gram_ref[base : base + 128, base : base + 128] = head
        gram_ref[base : base + 128, base + 128 : base + 256] = corner
        gram_ref[base + 128 : base + 256, base : base + 128] = corner.T
        gram_ref[base + 128 : base + 256, base + 128 : base + 256] = tail
        cross = block(384, 256)
        start = 256 + 128 * which
        gram_ref[0:256, start : start + 128] = cross
        gram_ref[start : start + 128, 0:256] = cross.T
    trace = jnp.where(diagonal(0, 0, (128, 128)), trace, 0.0)
    squares = jnp.sum(jnp.sum(trace, axis=0, keepdims=True), axis=1, keepdims=True)
    inverse = 1.0 / (jnp.sqrt(squares) + epsilon)
    gram = (gram_ref[...] * inverse) * inverse
    gram_ref[...] = gram
    gram_high[...], gram_low[...] = halves(gram)
    pair, first_pair = (gram_high, gram_low), (first_high, first_low)
    inner_pair, after_pair = (inner_high, inner_low), (after_high, after_low)

    def polynomial(square, rows, columns):
        unit = diagonal(rows.start, columns.start, square.shape)
        value = quintic_b * gram_ref[rows, columns] + quintic_c * square
        return value + jnp.where(unit, f32(quintic_a), f32(0.0))

    multiply(pair, pair, first_pair, polynomial)
    multiply(first_pair, pair, inner_pair, lambda value, rows, columns: value)
    multiply(first_pair, inner_pair, after_pair, lambda value, rows, columns: value)
    first_value = (first_high[...], first_low[...])
    after_value = (after_high[...], after_low[...])
    starts = [core * 256 + spot]
    for which in range(2):
        starts.append(256 * which + lax.rem(tensor, 4) * 64 + lax.div(tensor, 4) * 16)
    slab = tuple(
        jnp.concatenate([part[pl.ds(pl.multiple_of(start, 16), 16)] for start in starts], axis=0) for part in after_pair
    )
    units = jnp.concatenate([diagonal(start, 0, (16, IN)) for start in starts], axis=0)
    second = quintic_b * (slab[0].astype(f32) + slab[1].astype(f32))
    second = second + quintic_c * mul3(slab, after_value, NN) + jnp.where(units, f32(quintic_a), f32(0.0))
    second_pair = halves(second)
    own = tuple(part[0:16] for part in second_pair)
    total = mul3(own, first_value, NN)
    update = mul3(halves(total), halves(rows_ref[...].reshape(IN, 256)), NN) * inverse
    scale = learn_rate * 0.2 * float(max(IN, OUT)) ** 0.5
    new_weight_ref[...] = weight_ref[...] * (1.0 - learn_rate * weight_decay) - scale * update
    product = mul3(own, after_value, NN)
    final = mul3(halves(product), tuple(part[16:48] for part in second_pair), NT)
    identity = diagonal(lax.axis_index("dp") * 16, tensor * 32, (16, 32))
    residual_ref[...] = final - jnp.where(identity, f32(1.0), f32(0.0))


def call(kernel, outs, scratch=(), limit=4 << 20):
    return pl.pallas_call(
        kernel,
        out_shape=tuple(jax.ShapeDtypeStruct(shape, f32) for shape in outs),
        scratch_shapes=list(scratch),
        compiler_params=pltpu.CompilerParams(vmem_limit_bytes=limit),
    )


def exchange(value, axis, groups=None):
    return lax.all_to_all(value, axis, 0, 0, tiled=True, axis_index_groups=groups)


def per_device(gradients, momentum, weight):
    chunks = (4, 4, 16, 256)
    gradients = gradients.reshape(4, 4, 2, 16, 256)
    (send,) = call(send_kernel, [chunks])(gradients)
    (parts,) = call(core_sum_kernel, [chunks])(gradients, lax.ppermute(send, "dp", CORE))
    (parts,) = call(near_sum_kernel, [chunks[1:]])(exchange(parts, "dp", NEAR), momentum)
    parts = parts + lax.ppermute(parts, "dp", FAR[0])
    (spread,) = call(far_sum_kernel, [chunks])(parts, lax.ppermute(parts, "dp", FAR[1]))
    mine = exchange(spread, "dp", NEAR).reshape(256, 256)
    other = lax.ppermute(mine, "dp", CORE)
    blocks, rows = call(gram_kernel, [(640, 128), (2, 256, 256)], limit=8 << 20)(mine, other)
    (spread,) = call(tensor_sum_kernel, [(16, 40, 128)])(exchange(blocks.reshape(16, 40, 128), "tensor"))
    mine = exchange(spread, "tensor").reshape(640, 128)
    other = lax.ppermute(mine, "dp", CORE)
    return call(
        final_kernel,
        [(16, 256), (16, 256), (16, 32)],
        [pltpu.VMEM((IN, IN), f32)] + [pltpu.VMEM((IN, IN), bf16)] * 8,
        limit=24 << 20,
    )(mine, other, rows, weight)


def solution(mesh):
    return jax.shard_map(
        per_device,
        mesh=mesh,
        in_specs=(P("dp", None, "tensor"), P("dp", "tensor"), P("dp", "tensor")),
        out_specs=(P("dp", "tensor"), P("dp", "tensor"), P("dp", "tensor")),
        check_vma=False,
    )
```

```python
import jax
import jax.numpy as jnp
from jax import lax
from jax.experimental import pallas as pl
from jax.experimental.pallas import tpu as pltpu
from jax.sharding import PartitionSpec as P

IN = 512
OUT = 4096

decay_rate = 0.95
learn_rate = 0.02
weight_decay = 0.1
epsilon = 1e-07
quintic_a = 3.4445
quintic_b = -4.775
quintic_c = 2.0315

f32 = jnp.float32
bf16 = jnp.bfloat16

CORE = [(i, i ^ 1) for i in range(32)]
DOWN = [(i, i + 1) for i in range(0, 32, 2)]
BACK = [(i + 1, i) for i in range(0, 32, 2)]
BLOCKS = [(row, column) for row in range(4) for column in range(row, 4)]
NEAR = [[8 * far + 2 * near + core for near in range(4)] for far in range(4) for core in range(2)]
FAR = [[(i, i ^ (8 * steps[(i + i // 4) % 2])) for i in range(32)] for steps in ((1, 3), (3, 1))]

NT = (((1,), (1,)), ((), ()))
NN = (((1,), (0,)), ((), ()))


def place():
    index = lax.axis_index("dp")
    return lax.rem(lax.div(index, 2), 4), lax.div(index, 8), lax.rem(index, 2)


def halves(value):
    high = value.astype(bf16)
    low = (value - high.astype(f32)).astype(bf16)
    return high, low


def mul3(left, right, dims):
    dot = lambda x, y: lax.dot_general(x, y, dims, preferred_element_type=f32)
    return dot(left[0], right[0]) + (dot(left[0], right[1]) + dot(left[1], right[0]))


def send_kernel(grad_ref, send_ref):
    _, _, core = place()
    for near in range(4):
        for far in range(4):
            send_ref[near, far] = grad_ref[far, near, 1 - core].astype(f32)


def core_sum_kernel(grad_ref, got_ref, out_ref):
    _, _, core = place()
    for near in range(4):
        for far in range(4):
            out_ref[near, far] = grad_ref[far, near, core].astype(f32) + got_ref[near, far]


def near_sum_kernel(parts_ref, momentum_ref, out_ref):
    _, mine, _ = place()
    for far in range(4):
        total = (parts_ref[0, far] + parts_ref[1, far]) + (parts_ref[2, far] + parts_ref[3, far])
        out_ref[far] = total + jnp.where(mine == far, f32(decay_rate), f32(0.0)) * momentum_ref[...]


def far_sum_kernel(own_ref, other_ref, out_ref):
    for far in range(4):
        total = own_ref[far] + other_ref[far]
        for other in range(4):
            out_ref[other, far] = total


def gram_kernel(first_ref, last_ref, out_ref):
    pieces = [halves(ref[start : start + 128]) for ref in (first_ref, last_ref) for start in (0, 128)]
    for index, (row, column) in enumerate(BLOCKS):
        out_ref[128 * index : 128 * index + 128] = mul3(pieces[row], pieces[column], NT)


def tensor_sum_kernel(parts_ref, out_ref):
    total = parts_ref[0]
    for index in range(1, 16):
        total = total + parts_ref[index]
    for index in range(16):
        out_ref[index] = total


def diagonal(start_row, start_column, shape):
    rows = start_row + lax.broadcasted_iota(jnp.int32, shape, 0)
    columns = start_column + lax.broadcasted_iota(jnp.int32, shape, 1)
    return rows == columns


def multiply(left, right, out, change):
    top, low = slice(0, 256), slice(256, 512)
    pick = lambda pair, rows, columns: tuple(part[rows, columns] for part in pair)
    whole = slice(0, 512)
    upper = change(mul3(pick(left, top, whole), pick(right, whole, whole), NN), top, whole)
    lower = change(mul3(pick(left, low, whole), pick(right, whole, low), NN), low, low)
    out[0][top], out[1][top] = halves(upper)
    out[0][low, low], out[1][low, low] = halves(lower)
    out[0][low, top], out[1][low, top] = halves(upper[:, low].T)


def final_kernel(
    blocks_ref, first_ref, last_ref, own_ref, other_ref,
    gram_ref, gram_high, gram_low, first_high, first_low, inner_high, inner_low, after_high, after_low,
):
    near, far, _ = place()
    tensor = lax.axis_index("tensor")
    trace = jnp.zeros((128, 128), f32)
    for index, (row, column) in enumerate(BLOCKS):
        block = blocks_ref[128 * index : 128 * index + 128]
        gram_ref[128 * row : 128 * row + 128, 128 * column : 128 * column + 128] = block
        if row == column:
            trace = trace + block
        else:
            gram_ref[128 * column : 128 * column + 128, 128 * row : 128 * row + 128] = block.T
    trace = jnp.where(diagonal(0, 0, (128, 128)), trace, 0.0)
    squares = jnp.sum(jnp.sum(trace, axis=0, keepdims=True), axis=1, keepdims=True)
    inverse = 1.0 / (jnp.sqrt(squares) + epsilon)
    gram = (gram_ref[...] * inverse) * inverse
    gram_ref[...] = gram
    gram_high[...], gram_low[...] = halves(gram)
    pair, first_pair = (gram_high, gram_low), (first_high, first_low)
    inner_pair, after_pair = (inner_high, inner_low), (after_high, after_low)

    def polynomial(square, rows, columns):
        unit = diagonal(rows.start, columns.start, square.shape)
        value = quintic_b * gram_ref[rows, columns] + quintic_c * square
        return value + jnp.where(unit, f32(quintic_a), f32(0.0))

    multiply(pair, pair, first_pair, polynomial)
    multiply(first_pair, pair, inner_pair, lambda value, rows, columns: value)
    multiply(first_pair, inner_pair, after_pair, lambda value, rows, columns: value)
    first_value = (first_high[...], first_low[...])
    after_value = (after_high[...], after_low[...])
    spot = pl.multiple_of(near * 64 + far * 16, 16)
    column = pl.multiple_of(lax.rem(tensor, 4) * 64 + lax.div(tensor, 4) * 16, 16)
    starts = [pl.multiple_of(256 * side + start, 16) for start in (spot, column) for side in range(2)]
    slab = tuple(jnp.concatenate([part[pl.ds(start, 16)] for start in starts], axis=0) for part in after_pair)
    units = jnp.concatenate([diagonal(start, 0, (16, IN)) for start in starts], axis=0)
    second = quintic_b * (slab[0].astype(f32) + slab[1].astype(f32))
    second = second + quintic_c * mul3(slab, after_value, NN) + jnp.where(units, f32(quintic_a), f32(0.0))
    second_pair = halves(second)
    chip = tuple(part[0:32] for part in second_pair)
    total = mul3(chip, first_value, NN)
    scale = learn_rate * 0.2 * float(max(IN, OUT)) ** 0.5
    update = mul3(halves(total), halves(jnp.concatenate([first_ref[...], last_ref[...]], axis=0)), NN) * (inverse * scale)
    product = mul3(chip, after_value, NN)
    final = mul3(halves(product), tuple(part[32:64] for part in second_pair), NT)
    identity = diagonal(2 * spot, 2 * column, (32, 32))
    residual = final - jnp.where(identity, f32(1.0), f32(0.0))
    for side, (out_ref, rows_ref) in enumerate(((other_ref, first_ref), (own_ref, last_ref))):
        out_ref[0:16] = rows_ref[pl.ds(spot, 16)]
        out_ref[16:32] = update[16 * side : 16 * side + 16]
        out_ref[32:48, 0:32] = residual[16 * side : 16 * side + 16]
        out_ref[32:48, 32:256] = jnp.zeros((16, 224), f32)


def finish_kernel(own_ref, got_ref, weight_ref, new_momentum_ref, new_weight_ref, residual_ref):
    _, _, core = place()
    results = jnp.where(core == 1, own_ref[...], got_ref[...])
    new_momentum_ref[...] = results[0:16]
    new_weight_ref[...] = weight_ref[...] * (1.0 - learn_rate * weight_decay) - results[16:32]
    residual_ref[...] = results[32:48, 0:32]


def call(kernel, outs, scratch=(), limit=4 << 20):
    return pl.pallas_call(
        kernel,
        out_shape=tuple(jax.ShapeDtypeStruct(shape, f32) for shape in outs),
        scratch_shapes=list(scratch),
        compiler_params=pltpu.CompilerParams(vmem_limit_bytes=limit),
    )


def exchange(value, axis, groups=None):
    return lax.all_to_all(value, axis, 0, 0, tiled=True, axis_index_groups=groups)


def both_cores(first, last):
    split = (16, 80, 128)
    (value,) = call(gram_kernel, [(1280, 128)], limit=8 << 20)(first, last)
    (value,) = call(tensor_sum_kernel, [split])(exchange(value.reshape(split), "tensor"))
    return call(
        final_kernel,
        [(48, 256), (48, 256)],
        [pltpu.VMEM((IN, IN), f32)] + [pltpu.VMEM((IN, IN), bf16)] * 8,
        limit=24 << 20,
    )(exchange(value, "tensor").reshape(1280, 128), first, last)


def no_core(first, last):
    return jnp.zeros((48, 256), f32), jnp.zeros((48, 256), f32)


def per_device(gradients, momentum, weight):
    chunks = (4, 4, 16, 256)
    gradients = gradients.reshape(4, 4, 2, 16, 256)
    (send,) = call(send_kernel, [chunks])(gradients)
    (parts,) = call(core_sum_kernel, [chunks])(gradients, lax.ppermute(send, "dp", CORE))
    (parts,) = call(near_sum_kernel, [chunks[1:]])(exchange(parts, "dp", NEAR), momentum)
    parts = parts + lax.ppermute(parts, "dp", FAR[0])
    (spread,) = call(far_sum_kernel, [chunks])(parts, lax.ppermute(parts, "dp", FAR[1]))
    mine = exchange(spread, "dp", NEAR).reshape(256, 256)
    first = lax.ppermute(mine, "dp", DOWN)
    own, other = lax.cond(place()[2] == 1, both_cores, no_core, first, mine)
    return call(finish_kernel, [(16, 256), (16, 256), (16, 32)])(own, lax.ppermute(other, "dp", BACK), weight)


def solution(mesh):
    return jax.shard_map(
        per_device,
        mesh=mesh,
        in_specs=(P("dp", None, "tensor"), P("dp", "tensor"), P("dp", "tensor")),
        out_specs=(P("dp", "tensor"), P("dp", "tensor"), P("dp", "tensor")),
        check_vma=False,
    )
```

```python
import jax
import jax.numpy as jnp
from jax import lax
from jax.experimental import pallas as pl
from jax.experimental.pallas import tpu as pltpu
from jax.sharding import PartitionSpec as P

IN = 512
OUT = 4096

decay_rate = 0.95
learn_rate = 0.02
weight_decay = 0.1
epsilon = 1e-07
quintic_a = 3.4445
quintic_b = -4.775
quintic_c = 2.0315

f32 = jnp.float32
bf16 = jnp.bfloat16

CORE = [(i, i ^ 1) for i in range(32)]
DOWN = [[(i, (i + 1) ^ (2 * step)) for i in range(0, 32, 2)] for step in range(4)]
BACK = [(i + 1, i) for i in range(0, 32, 2)]
BLOCKS = [(row, column) for row in range(4) for column in range(row, 4)]
NEAR = [[8 * far + 2 * near + core for near in range(4)] for far in range(4) for core in range(2)]
FAR = [[(i, i ^ (8 * steps[(i + i // 4) % 2])) for i in range(32)] for steps in ((1, 3), (3, 1))]

NT = (((1,), (1,)), ((), ()))
NN = (((1,), (0,)), ((), ()))


def place():
    index = lax.axis_index("dp")
    return lax.rem(lax.div(index, 2), 4), lax.div(index, 8), lax.rem(index, 2)


def halves(value):
    high = value.astype(bf16)
    low = (value - high.astype(f32)).astype(bf16)
    return high, low


def mul3(left, right, dims):
    dot = lambda x, y: lax.dot_general(x, y, dims, preferred_element_type=f32)
    return dot(left[0], right[0]) + (dot(left[0], right[1]) + dot(left[1], right[0]))


def send_kernel(grad_ref, send_ref):
    _, _, core = place()
    for near in range(4):
        for far in range(4):
            send_ref[near, far] = grad_ref[far, near, 1 - core].astype(f32)


def core_sum_kernel(grad_ref, got_ref, out_ref):
    _, _, core = place()
    for near in range(4):
        for far in range(4):
            out_ref[near, far] = grad_ref[far, near, core].astype(f32) + got_ref[near, far]


def near_sum_kernel(parts_ref, momentum_ref, out_ref):
    _, mine, _ = place()
    for far in range(4):
        total = (parts_ref[0, far] + parts_ref[1, far]) + (parts_ref[2, far] + parts_ref[3, far])
        out_ref[far] = total + jnp.where(mine == far, f32(decay_rate), f32(0.0)) * momentum_ref[...]


def far_sum_kernel(own_ref, other_ref, out_ref):
    for far in range(4):
        total = own_ref[far] + other_ref[far]
        for other in range(4):
            out_ref[other, far] = total


def far_part_kernel(own_ref, other_ref, out_ref):
    out_ref[...] = own_ref[...] + other_ref[...]


def gram_kernel(last_ref, part_0, part_1, part_2, part_3, out_ref, first_ref):
    near, _, _ = place()
    for step, part_ref in enumerate((part_0, part_1, part_2, part_3)):
        start = pl.multiple_of((near ^ step) * 64, 64)
        first_ref[pl.ds(start, 64)] = part_ref[...].reshape(64, 256)
    pieces = [halves(ref[start : start + 128]) for ref in (first_ref, last_ref) for start in (0, 128)]
    for index, (row, column) in enumerate(BLOCKS):
        out_ref[128 * index : 128 * index + 128] = mul3(pieces[row], pieces[column], NT)


def tensor_sum_kernel(parts_ref, out_ref):
    total = parts_ref[0]
    for index in range(1, 16):
        total = total + parts_ref[index]
    for index in range(16):
        out_ref[index] = total


def diagonal(start_row, start_column, shape):
    rows = start_row + lax.broadcasted_iota(jnp.int32, shape, 0)
    columns = start_column + lax.broadcasted_iota(jnp.int32, shape, 1)
    return rows == columns


def multiply(left, right, out, change):
    top, low = slice(0, 256), slice(256, 512)
    pick = lambda pair, rows, columns: tuple(part[rows, columns] for part in pair)
    whole = slice(0, 512)
    upper = change(mul3(pick(left, top, whole), pick(right, whole, whole), NN), top, whole)
    lower = change(mul3(pick(left, low, whole), pick(right, whole, low), NN), low, low)
    out[0][top], out[1][top] = halves(upper)
    out[0][low, low], out[1][low, low] = halves(lower)
    out[0][low, top], out[1][low, top] = halves(upper[:, low].T)


def final_kernel(
    blocks_ref, first_ref, last_ref, own_ref, other_ref,
    gram_ref, gram_high, gram_low, first_high, first_low, inner_high, inner_low, after_high, after_low,
):
    near, far, _ = place()
    tensor = lax.axis_index("tensor")
    trace = jnp.zeros((128, 128), f32)
    for index, (row, column) in enumerate(BLOCKS):
        block = blocks_ref[128 * index : 128 * index + 128]
        gram_ref[128 * row : 128 * row + 128, 128 * column : 128 * column + 128] = block
        if row == column:
            trace = trace + block
        else:
            gram_ref[128 * column : 128 * column + 128, 128 * row : 128 * row + 128] = block.T
    trace = jnp.where(diagonal(0, 0, (128, 128)), trace, 0.0)
    squares = jnp.sum(jnp.sum(trace, axis=0, keepdims=True), axis=1, keepdims=True)
    inverse = 1.0 / (jnp.sqrt(squares) + epsilon)
    gram = (gram_ref[...] * inverse) * inverse
    gram_ref[...] = gram
    gram_high[...], gram_low[...] = halves(gram)
    pair, first_pair = (gram_high, gram_low), (first_high, first_low)
    inner_pair, after_pair = (inner_high, inner_low), (after_high, after_low)

    def polynomial(square, rows, columns):
        unit = diagonal(rows.start, columns.start, square.shape)
        value = quintic_b * gram_ref[rows, columns] + quintic_c * square
        return value + jnp.where(unit, f32(quintic_a), f32(0.0))

    multiply(pair, pair, first_pair, polynomial)
    multiply(first_pair, pair, inner_pair, lambda value, rows, columns: value)
    multiply(first_pair, inner_pair, after_pair, lambda value, rows, columns: value)
    first_value = (first_high[...], first_low[...])
    after_value = (after_high[...], after_low[...])
    spot = pl.multiple_of(near * 64 + far * 16, 16)
    column = pl.multiple_of(lax.rem(tensor, 4) * 64 + lax.div(tensor, 4) * 16, 16)
    starts = [pl.multiple_of(256 * side + start, 16) for start in (spot, column) for side in range(2)]
    slab = tuple(jnp.concatenate([part[pl.ds(start, 16)] for start in starts], axis=0) for part in after_pair)
    units = jnp.concatenate([diagonal(start, 0, (16, IN)) for start in starts], axis=0)
    second = quintic_b * (slab[0].astype(f32) + slab[1].astype(f32))
    second = second + quintic_c * mul3(slab, after_value, NN) + jnp.where(units, f32(quintic_a), f32(0.0))
    second_pair = halves(second)
    chip = tuple(part[0:32] for part in second_pair)
    total = mul3(chip, first_value, NN)
    scale = learn_rate * 0.2 * float(max(IN, OUT)) ** 0.5
    update = mul3(halves(total), halves(jnp.concatenate([first_ref[...], last_ref[...]], axis=0)), NN) * (inverse * scale)
    product = mul3(chip, after_value, NN)
    final = mul3(halves(product), tuple(part[32:64] for part in second_pair), NT)
    identity = diagonal(2 * spot, 2 * column, (32, 32))
    residual = final - jnp.where(identity, f32(1.0), f32(0.0))
    for side, (out_ref, rows_ref) in enumerate(((other_ref, first_ref), (own_ref, last_ref))):
        out_ref[0:16] = rows_ref[pl.ds(spot, 16)]
        out_ref[16:32] = update[16 * side : 16 * side + 16]
        out_ref[32:48, 0:32] = residual[16 * side : 16 * side + 16]
        out_ref[32:48, 32:256] = jnp.zeros((16, 224), f32)


def finish_kernel(own_ref, got_ref, weight_ref, new_momentum_ref, new_weight_ref, residual_ref):
    _, _, core = place()
    results = jnp.where(core == 1, own_ref[...], got_ref[...])
    new_momentum_ref[...] = results[0:16]
    new_weight_ref[...] = weight_ref[...] * (1.0 - learn_rate * weight_decay) - results[16:32]
    residual_ref[...] = results[32:48, 0:32]


def call(kernel, outs, scratch=(), limit=4 << 20):
    return pl.pallas_call(
        kernel,
        out_shape=tuple(jax.ShapeDtypeStruct(shape, f32) for shape in outs),
        scratch_shapes=list(scratch),
        compiler_params=pltpu.CompilerParams(vmem_limit_bytes=limit),
    )


def exchange(value, axis, groups=None):
    return lax.all_to_all(value, axis, 0, 0, tiled=True, axis_index_groups=groups)


def near_gather(own, other):
    (spread,) = call(far_sum_kernel, [(4, 4, 16, 256)])(own, other)
    return exchange(spread, "dp", NEAR).reshape(256, 256)


def no_gather(own, other):
    return jnp.zeros((256, 256), f32)


def both_cores(last, *parts):
    split = (16, 80, 128)
    value, first = call(gram_kernel, [(1280, 128), (256, 256)], limit=8 << 20)(last, *parts)
    (value,) = call(tensor_sum_kernel, [split])(exchange(value.reshape(split), "tensor"))
    return call(
        final_kernel,
        [(48, 256), (48, 256)],
        [pltpu.VMEM((IN, IN), f32)] + [pltpu.VMEM((IN, IN), bf16)] * 8,
        limit=24 << 20,
    )(exchange(value, "tensor").reshape(1280, 128), first, last)


def no_core(last, *parts):
    return jnp.zeros((48, 256), f32), jnp.zeros((48, 256), f32)


def per_device(gradients, momentum, weight):
    chunks = (4, 4, 16, 256)
    gradients = gradients.reshape(4, 4, 2, 16, 256)
    (send,) = call(send_kernel, [chunks])(gradients)
    (parts,) = call(core_sum_kernel, [chunks])(gradients, lax.ppermute(send, "dp", CORE))
    (parts,) = call(near_sum_kernel, [chunks[1:]])(exchange(parts, "dp", NEAR), momentum)
    parts = parts + lax.ppermute(parts, "dp", FAR[0])
    other = lax.ppermute(parts, "dp", FAR[1])
    (part,) = call(far_part_kernel, [chunks[1:]])(parts, other)
    pieces = [lax.ppermute(part, "dp", pairs) for pairs in DOWN]
    last = lax.cond(place()[2] == 1, near_gather, no_gather, parts, other)
    own, other = lax.cond(place()[2] == 1, both_cores, no_core, last, *pieces)
    return call(finish_kernel, [(16, 256), (16, 256), (16, 32)])(own, lax.ppermute(other, "dp", BACK), weight)


def solution(mesh):
    return jax.shard_map(
        per_device,
        mesh=mesh,
        in_specs=(P("dp", None, "tensor"), P("dp", "tensor"), P("dp", "tensor")),
        out_specs=(P("dp", "tensor"), P("dp", "tensor"), P("dp", "tensor")),
        check_vma=False,
    )
```

```python
import jax
import jax.numpy as jnp
from jax import lax
from jax.experimental import pallas as pl
from jax.experimental.pallas import tpu as pltpu
from jax.sharding import PartitionSpec as P

IN = 512
OUT = 4096

decay_rate = 0.95
learn_rate = 0.02
weight_decay = 0.1
epsilon = 1e-07
quintic_a = 3.4445
quintic_b = -4.775
quintic_c = 2.0315

f32 = jnp.float32
bf16 = jnp.bfloat16

CORE = [(i, i ^ 1) for i in range(32)]
DOWN = [[(i, (i + 1) ^ (2 * step)) for i in range(0, 32, 2)] for step in range(4)]
BACK = [(i + 1, i) for i in range(0, 32, 2)]
BLOCKS = [(row, column) for row in range(4) for column in range(row, 4)]
NEAR = [[8 * far + 2 * near + core for near in range(4)] for far in range(4) for core in range(2)]
FAR = [[(i, i ^ (8 * steps[(i + i // 4) % 2])) for i in range(32)] for steps in ((1, 3), (3, 1))]

NT = (((1,), (1,)), ((), ()))
NN = (((1,), (0,)), ((), ()))


def place():
    index = lax.axis_index("dp")
    return lax.rem(lax.div(index, 2), 4), lax.div(index, 8), lax.rem(index, 2)


def halves(value):
    high = value.astype(bf16)
    low = (value - high.astype(f32)).astype(bf16)
    return high, low


def mul3(left, right, dims):
    dot = lambda x, y: lax.dot_general(x, y, dims, preferred_element_type=f32)
    return dot(left[0], right[0]) + (dot(left[0], right[1]) + dot(left[1], right[0]))


def send_kernel(grad_ref, send_ref):
    _, _, core = place()
    for near in range(4):
        for far in range(4):
            send_ref[near, far] = grad_ref[far, near, 1 - core].astype(f32)


def core_sum_kernel(grad_ref, up_ref, down_ref, out_ref):
    _, _, core = place()
    for near in range(4):
        for far in range(4):
            out_ref[near, far] = grad_ref[far, near, core].astype(f32) + (up_ref[near, far] + down_ref[near, far])


def near_sum_kernel(parts_ref, momentum_ref, out_ref):
    _, mine, _ = place()
    for far in range(4):
        total = (parts_ref[0, far] + parts_ref[1, far]) + (parts_ref[2, far] + parts_ref[3, far])
        out_ref[far] = total + jnp.where(mine == far, f32(decay_rate), f32(0.0)) * momentum_ref[...]


def far_sum_kernel(own_ref, other_ref, out_ref):
    for far in range(4):
        total = own_ref[far] + other_ref[far]
        for other in range(4):
            out_ref[other, far] = total


def far_part_kernel(own_ref, other_ref, out_ref):
    out_ref[...] = own_ref[...] + other_ref[...]


def gram_kernel(last_ref, part_0, part_1, part_2, part_3, out_ref, first_ref):
    near, _, _ = place()
    for step, part_ref in enumerate((part_0, part_1, part_2, part_3)):
        start = pl.multiple_of((near ^ step) * 64, 64)
        first_ref[pl.ds(start, 64)] = part_ref[...].reshape(64, 256)
    pieces = [halves(ref[start : start + 128]) for ref in (first_ref, last_ref) for start in (0, 128)]
    for index, (row, column) in enumerate(BLOCKS):
        out_ref[128 * index : 128 * index + 128] = mul3(pieces[row], pieces[column], NT)


def tensor_sum_kernel(parts_ref, out_ref):
    total = parts_ref[0]
    for index in range(1, 16):
        total = total + parts_ref[index]
    for index in range(16):
        out_ref[index] = total


def diagonal(start_row, start_column, shape):
    rows = start_row + lax.broadcasted_iota(jnp.int32, shape, 0)
    columns = start_column + lax.broadcasted_iota(jnp.int32, shape, 1)
    return rows == columns


def multiply(left, right, out, change):
    top, low = slice(0, 256), slice(256, 512)
    pick = lambda pair, rows, columns: tuple(part[rows, columns] for part in pair)
    whole = slice(0, 512)
    upper = change(mul3(pick(left, top, whole), pick(right, whole, whole), NN), top, whole)
    lower = change(mul3(pick(left, low, whole), pick(right, whole, low), NN), low, low)
    out[0][top], out[1][top] = halves(upper)
    out[0][low, low], out[1][low, low] = halves(lower)
    out[0][low, top], out[1][low, top] = halves(upper[:, low].T)


def final_kernel(
    blocks_ref, first_ref, last_ref, own_ref, other_ref,
    gram_ref, gram_high, gram_low, first_high, first_low, inner_high, inner_low, after_high, after_low,
):
    near, far, _ = place()
    tensor = lax.axis_index("tensor")
    trace = jnp.zeros((128, 128), f32)
    for index, (row, column) in enumerate(BLOCKS):
        block = blocks_ref[128 * index : 128 * index + 128]
        gram_ref[128 * row : 128 * row + 128, 128 * column : 128 * column + 128] = block
        if row == column:
            trace = trace + block
        else:
            gram_ref[128 * column : 128 * column + 128, 128 * row : 128 * row + 128] = block.T
    trace = jnp.where(diagonal(0, 0, (128, 128)), trace, 0.0)
    squares = jnp.sum(jnp.sum(trace, axis=0, keepdims=True), axis=1, keepdims=True)
    inverse = 1.0 / (jnp.sqrt(squares) + epsilon)
    gram = (gram_ref[...] * inverse) * inverse
    gram_ref[...] = gram
    gram_high[...], gram_low[...] = halves(gram)
    pair, first_pair = (gram_high, gram_low), (first_high, first_low)
    inner_pair, after_pair = (inner_high, inner_low), (after_high, after_low)

    def polynomial(square, rows, columns):
        unit = diagonal(rows.start, columns.start, square.shape)
        value = quintic_b * gram_ref[rows, columns] + quintic_c * square
        return value + jnp.where(unit, f32(quintic_a), f32(0.0))

    multiply(pair, pair, first_pair, polynomial)
    multiply(first_pair, pair, inner_pair, lambda value, rows, columns: value)
    multiply(first_pair, inner_pair, after_pair, lambda value, rows, columns: value)
    first_value = (first_high[...], first_low[...])
    after_value = (after_high[...], after_low[...])
    spot = pl.multiple_of(near * 64 + far * 16, 16)
    column = pl.multiple_of(lax.rem(tensor, 4) * 64 + lax.div(tensor, 4) * 16, 16)
    starts = [pl.multiple_of(256 * side + start, 16) for start in (spot, column) for side in range(2)]
    slab = tuple(jnp.concatenate([part[pl.ds(start, 16)] for start in starts], axis=0) for part in after_pair)
    units = jnp.concatenate([diagonal(start, 0, (16, IN)) for start in starts], axis=0)
    second = quintic_b * (slab[0].astype(f32) + slab[1].astype(f32))
    second = second + quintic_c * mul3(slab, after_value, NN) + jnp.where(units, f32(quintic_a), f32(0.0))
    second_pair = halves(second)
    chip = tuple(part[0:32] for part in second_pair)
    total = mul3(chip, first_value, NN)
    scale = learn_rate * 0.2 * float(max(IN, OUT)) ** 0.5
    update = mul3(halves(total), halves(jnp.concatenate([first_ref[...], last_ref[...]], axis=0)), NN) * (inverse * scale)
    product = mul3(chip, after_value, NN)
    final = mul3(halves(product), tuple(part[32:64] for part in second_pair), NT)
    identity = diagonal(2 * spot, 2 * column, (32, 32))
    residual = final - jnp.where(identity, f32(1.0), f32(0.0))
    for side, (out_ref, rows_ref) in enumerate(((other_ref, first_ref), (own_ref, last_ref))):
        out_ref[0:16] = rows_ref[pl.ds(spot, 16)]
        out_ref[16:32] = update[16 * side : 16 * side + 16]
        out_ref[32:48, 0:32] = residual[16 * side : 16 * side + 16]
        out_ref[32:48, 32:256] = jnp.zeros((16, 224), f32)


def finish_kernel(own_ref, got_ref, weight_ref, new_momentum_ref, new_weight_ref, residual_ref):
    _, _, core = place()
    results = jnp.where(core == 1, own_ref[...], got_ref[...])
    new_momentum_ref[...] = results[0:16]
    new_weight_ref[...] = weight_ref[...] * (1.0 - learn_rate * weight_decay) - results[16:32]
    residual_ref[...] = results[32:48, 0:32]


def call(kernel, outs, scratch=(), limit=4 << 20):
    return pl.pallas_call(
        kernel,
        out_shape=tuple(jax.ShapeDtypeStruct(shape, f32) for shape in outs),
        scratch_shapes=list(scratch),
        compiler_params=pltpu.CompilerParams(vmem_limit_bytes=limit),
    )


def exchange(value, axis, groups=None):
    return lax.all_to_all(value, axis, 0, 0, tiled=True, axis_index_groups=groups)


def near_gather(own, other):
    (spread,) = call(far_sum_kernel, [(4, 4, 16, 256)])(own, other)
    return exchange(spread, "dp", NEAR).reshape(256, 256)


def no_gather(own, other):
    return jnp.zeros((256, 256), f32)


def both_cores(last, *parts):
    split = (16, 80, 128)
    value, first = call(gram_kernel, [(1280, 128), (256, 256)], limit=8 << 20)(last, *parts)
    (value,) = call(tensor_sum_kernel, [split])(exchange(value.reshape(split), "tensor"))
    return call(
        final_kernel,
        [(48, 256), (48, 256)],
        [pltpu.VMEM((IN, IN), f32)] + [pltpu.VMEM((IN, IN), bf16)] * 8,
        limit=24 << 20,
    )(exchange(value, "tensor").reshape(1280, 128), first, last)


def no_core(last, *parts):
    return jnp.zeros((48, 256), f32), jnp.zeros((48, 256), f32)


def per_device(gradients, momentum, weight):
    chunks = (4, 4, 16, 256)
    gradients = gradients.reshape(4, 4, 2, 16, 256)
    (send,) = call(send_kernel, [chunks])(gradients)
    (parts,) = call(core_sum_kernel, [chunks])(
        gradients, lax.ppermute(send, "dp", BACK), lax.ppermute(send, "dp", DOWN[0])
    )
    (parts,) = call(near_sum_kernel, [chunks[1:]])(exchange(parts, "dp", NEAR), momentum)
    parts = parts + lax.ppermute(parts, "dp", FAR[0])
    other = lax.ppermute(parts, "dp", FAR[1])
    (part,) = call(far_part_kernel, [chunks[1:]])(parts, other)
    pieces = [lax.ppermute(part, "dp", pairs) for pairs in DOWN]
    last = lax.cond(place()[2] == 1, near_gather, no_gather, parts, other)
    own, other = lax.cond(place()[2] == 1, both_cores, no_core, last, *pieces)
    return call(finish_kernel, [(16, 256), (16, 256), (16, 32)])(own, lax.ppermute(other, "dp", BACK), weight)


def solution(mesh):
    return jax.shard_map(
        per_device,
        mesh=mesh,
        in_specs=(P("dp", None, "tensor"), P("dp", "tensor"), P("dp", "tensor")),
        out_specs=(P("dp", "tensor"), P("dp", "tensor"), P("dp", "tensor")),
        check_vma=False,
    )
```

```python
import jax
import jax.numpy as jnp
from jax import lax
from jax.experimental import pallas as pl
from jax.experimental.pallas import tpu as pltpu
from jax.sharding import PartitionSpec as P

IN = 512
OUT = 4096

decay_rate = 0.95
learn_rate = 0.02
weight_decay = 0.1
epsilon = 1e-07
quintic_a = 3.4445
quintic_b = -4.775
quintic_c = 2.0315

f32 = jnp.float32
bf16 = jnp.bfloat16

CORE = [(i, i ^ 1) for i in range(32)]
DOWN = [[(i, (i + 1) ^ (2 * step)) for i in range(0, 32, 2)] for step in range(4)]
BACK = [(i + 1, i) for i in range(0, 32, 2)]
BLOCKS = [(row, column) for row in range(4) for column in range(row, 4)]
NEAR = [[8 * far + 2 * near + core for near in range(4)] for far in range(4) for core in range(2)]
FAR = [[(i, i ^ (8 * steps[(1 + i + i // 4) % 2])) for i in range(32)] for steps in ((1, 3), (3, 1))]

NT = (((1,), (1,)), ((), ()))
NN = (((1,), (0,)), ((), ()))


def place():
    index = lax.axis_index("dp")
    return lax.rem(lax.div(index, 2), 4), lax.div(index, 8), lax.rem(index, 2)


def halves(value):
    high = value.astype(bf16)
    low = (value - high.astype(f32)).astype(bf16)
    return high, low


def mul3(left, right, dims):
    dot = lambda x, y: lax.dot_general(x, y, dims, preferred_element_type=f32)
    return dot(left[0], right[0]) + (dot(left[0], right[1]) + dot(left[1], right[0]))


def send_kernel(grad_ref, send_ref):
    _, _, core = place()
    for near in range(4):
        for far in range(4):
            send_ref[near, far] = grad_ref[far, near, 1 - core].astype(f32)


def core_sum_kernel(grad_ref, got_ref, out_ref):
    _, _, core = place()
    for near in range(4):
        for far in range(4):
            out_ref[near, far] = grad_ref[far, near, core].astype(f32) + got_ref[near, far]


def near_sum_kernel(parts_ref, momentum_ref, out_ref):
    _, mine, _ = place()
    for far in range(4):
        total = (parts_ref[0, far] + parts_ref[1, far]) + (parts_ref[2, far] + parts_ref[3, far])
        out_ref[far] = total + jnp.where(mine == far, f32(decay_rate), f32(0.0)) * momentum_ref[...]


def far_sum_kernel(own_ref, other_ref, out_ref):
    for far in range(4):
        total = own_ref[far] + other_ref[far]
        for other in range(4):
            out_ref[other, far] = total


def far_part_kernel(own_ref, other_ref, out_ref):
    out_ref[...] = own_ref[...] + other_ref[...]


def gram_kernel(last_ref, part_0, part_1, part_2, part_3, out_ref, first_ref):
    near, _, _ = place()
    for step, part_ref in enumerate((part_0, part_1, part_2, part_3)):
        start = pl.multiple_of((near ^ step) * 64, 64)
        first_ref[pl.ds(start, 64)] = part_ref[...].reshape(64, 256)
    pieces = [halves(ref[start : start + 128]) for ref in (first_ref, last_ref) for start in (0, 128)]
    for index, (row, column) in enumerate(BLOCKS):
        out_ref[128 * index : 128 * index + 128] = mul3(pieces[row], pieces[column], NT)


def tensor_sum_kernel(parts_ref, out_ref):
    total = parts_ref[0]
    for index in range(1, 16):
        total = total + parts_ref[index]
    for index in range(16):
        out_ref[index] = total


def diagonal(start_row, start_column, shape):
    rows = start_row + lax.broadcasted_iota(jnp.int32, shape, 0)
    columns = start_column + lax.broadcasted_iota(jnp.int32, shape, 1)
    return rows == columns


def multiply(left, right, out, change):
    top, low = slice(0, 256), slice(256, 512)
    pick = lambda pair, rows, columns: tuple(part[rows, columns] for part in pair)
    whole = slice(0, 512)
    upper = change(mul3(pick(left, top, whole), pick(right, whole, whole), NN), top, whole)
    lower = change(mul3(pick(left, low, whole), pick(right, whole, low), NN), low, low)
    out[0][top], out[1][top] = halves(upper)
    out[0][low, low], out[1][low, low] = halves(lower)
    out[0][low, top], out[1][low, top] = halves(upper[:, low].T)


def final_kernel(
    blocks_ref, first_ref, last_ref, own_ref, other_ref,
    gram_ref, gram_high, gram_low, first_high, first_low, inner_high, inner_low, after_high, after_low,
):
    near, far, _ = place()
    tensor = lax.axis_index("tensor")
    trace = jnp.zeros((128, 128), f32)
    for index, (row, column) in enumerate(BLOCKS):
        block = blocks_ref[128 * index : 128 * index + 128]
        gram_ref[128 * row : 128 * row + 128, 128 * column : 128 * column + 128] = block
        if row == column:
            trace = trace + block
        else:
            gram_ref[128 * column : 128 * column + 128, 128 * row : 128 * row + 128] = block.T
    trace = jnp.where(diagonal(0, 0, (128, 128)), trace, 0.0)
    squares = jnp.sum(jnp.sum(trace, axis=0, keepdims=True), axis=1, keepdims=True)
    inverse = 1.0 / (jnp.sqrt(squares) + epsilon)
    gram = (gram_ref[...] * inverse) * inverse
    gram_ref[...] = gram
    gram_high[...], gram_low[...] = halves(gram)
    pair, first_pair = (gram_high, gram_low), (first_high, first_low)
    inner_pair, after_pair = (inner_high, inner_low), (after_high, after_low)

    def polynomial(square, rows, columns):
        unit = diagonal(rows.start, columns.start, square.shape)
        value = quintic_b * gram_ref[rows, columns] + quintic_c * square
        return value + jnp.where(unit, f32(quintic_a), f32(0.0))

    multiply(pair, pair, first_pair, polynomial)
    multiply(first_pair, pair, inner_pair, lambda value, rows, columns: value)
    multiply(first_pair, inner_pair, after_pair, lambda value, rows, columns: value)
    first_value = (first_high[...], first_low[...])
    after_value = (after_high[...], after_low[...])
    spot = pl.multiple_of(near * 64 + far * 16, 16)
    column = pl.multiple_of(lax.rem(tensor, 4) * 64 + lax.div(tensor, 4) * 16, 16)
    starts = [pl.multiple_of(256 * side + start, 16) for start in (spot, column) for side in range(2)]
    slab = tuple(jnp.concatenate([part[pl.ds(start, 16)] for start in starts], axis=0) for part in after_pair)
    units = jnp.concatenate([diagonal(start, 0, (16, IN)) for start in starts], axis=0)
    second = quintic_b * (slab[0].astype(f32) + slab[1].astype(f32))
    second = second + quintic_c * mul3(slab, after_value, NN) + jnp.where(units, f32(quintic_a), f32(0.0))
    second_pair = halves(second)
    chip = tuple(part[0:32] for part in second_pair)
    total = mul3(chip, first_value, NN)
    scale = learn_rate * 0.2 * float(max(IN, OUT)) ** 0.5
    update = mul3(halves(total), halves(jnp.concatenate([first_ref[...], last_ref[...]], axis=0)), NN) * (inverse * scale)
    product = mul3(chip, after_value, NN)
    final = mul3(halves(product), tuple(part[32:64] for part in second_pair), NT)
    identity = diagonal(2 * spot, 2 * column, (32, 32))
    residual = final - jnp.where(identity, f32(1.0), f32(0.0))
    for side, (out_ref, rows_ref) in enumerate(((other_ref, first_ref), (own_ref, last_ref))):
        out_ref[0:16] = rows_ref[pl.ds(spot, 16)]
        out_ref[16:32] = update[16 * side : 16 * side + 16]
        out_ref[32:48, 0:32] = residual[16 * side : 16 * side + 16]
        out_ref[32:48, 32:256] = jnp.zeros((16, 224), f32)


def finish_kernel(own_ref, got_ref, weight_ref, new_momentum_ref, new_weight_ref, residual_ref):
    _, _, core = place()
    results = jnp.where(core == 1, own_ref[...], got_ref[...])
    new_momentum_ref[...] = results[0:16]
    new_weight_ref[...] = weight_ref[...] * (1.0 - learn_rate * weight_decay) - results[16:32]
    residual_ref[...] = results[32:48, 0:32]


def call(kernel, outs, scratch=(), limit=4 << 20):
    return pl.pallas_call(
        kernel,
        out_shape=tuple(jax.ShapeDtypeStruct(shape, f32) for shape in outs),
        scratch_shapes=list(scratch),
        compiler_params=pltpu.CompilerParams(vmem_limit_bytes=limit),
    )


def exchange(value, axis, groups=None):
    return lax.all_to_all(value, axis, 0, 0, tiled=True, axis_index_groups=groups)


def near_gather(own, other):
    (spread,) = call(far_sum_kernel, [(4, 4, 16, 256)])(own, other)
    return exchange(spread, "dp", NEAR).reshape(256, 256)


def no_gather(own, other):
    return jnp.zeros((256, 256), f32)


def both_cores(last, *parts):
    split = (16, 80, 128)
    value, first = call(gram_kernel, [(1280, 128), (256, 256)], limit=8 << 20)(last, *parts)
    (value,) = call(tensor_sum_kernel, [split])(exchange(value.reshape(split), "tensor"))
    return call(
        final_kernel,
        [(48, 256), (48, 256)],
        [pltpu.VMEM((IN, IN), f32)] + [pltpu.VMEM((IN, IN), bf16)] * 8,
        limit=24 << 20,
    )(exchange(value, "tensor").reshape(1280, 128), first, last)


def no_core(last, *parts):
    return jnp.zeros((48, 256), f32), jnp.zeros((48, 256), f32)


def per_device(gradients, momentum, weight):
    chunks = (4, 4, 16, 256)
    gradients = gradients.reshape(4, 4, 2, 16, 256)
    (send,) = call(send_kernel, [chunks])(gradients)
    (parts,) = call(core_sum_kernel, [chunks])(gradients, lax.ppermute(send, "dp", CORE))
    (parts,) = call(near_sum_kernel, [chunks[1:]])(exchange(parts, "dp", NEAR), momentum)
    parts = parts + lax.ppermute(parts, "dp", FAR[0])
    other = lax.ppermute(parts, "dp", FAR[1])
    (part,) = call(far_part_kernel, [chunks[1:]])(parts, other)
    pieces = [lax.ppermute(part, "dp", pairs) for pairs in DOWN]
    last = lax.cond(place()[2] == 1, near_gather, no_gather, parts, other)
    own, other = lax.cond(place()[2] == 1, both_cores, no_core, last, *pieces)
    return call(finish_kernel, [(16, 256), (16, 256), (16, 32)])(own, lax.ppermute(other, "dp", BACK), weight)


def solution(mesh):
    return jax.shard_map(
        per_device,
        mesh=mesh,
        in_specs=(P("dp", None, "tensor"), P("dp", "tensor"), P("dp", "tensor")),
        out_specs=(P("dp", "tensor"), P("dp", "tensor"), P("dp", "tensor")),
        check_vma=False,
    )
```
